768 devices in a mesh: dp: 24 (over x_hi, z), graph: 32 (over x_lo, y, core).
Axes of the slice: x: 4 (x_hi: 2, x_lo: 2; x = x_hi * 2 + x_lo), y: 8, z: 12, core: 2. Of those that a mesh axis runs over, the one named last changes fastest.
Arguments:
- atom_h: bfloat16 [24, 256, 1024], P('dp', 'graph'), may hold values from -6 to 6
- edge_x: bfloat16 [24, 16384, 1024], P('dp', 'graph'), may hold values from -6 to 6
- edge_source: int32 [24, 16384], P('dp', 'graph'), may hold values from 0 to 255, as said below
- edge_target: int32 [24, 16384], P('dp', 'graph'), may hold values from 0 to 255, as said below
- trip_in: int32 [24, 32768], P('dp', 'graph'), may hold values from 0 to 16383, as said below
- trip_out: int32 [24, 32768], P('dp', 'graph'), may hold values from 0 to 16383, as said below
- basis: bfloat16 [24, 64, 32768], P('dp', None, 'graph'), may hold values from -6 to 6
- block_counts: int32 [24, 32], P('dp', 'graph'), may hold values from 2 to 8, as said below
- atom_cotangent: bfloat16 [24, 256, 1024], P('dp', 'graph'), may hold values from -6 to 6
- weight_edge: bfloat16 [1024, 1024], replicated, may hold values from -0.1875 to 0.1875
- weight_basis: bfloat16 [64, 1024], replicated, may hold values from -0.75 to 0.75
Outputs:
- grad_x: bfloat16 [24, 16384, 1024], P('dp', 'graph')
- grad_h: bfloat16 [24, 256, 1024], P('dp', 'graph')
- grad_weight_edge: float32 [1024, 1024], P('graph')
- grad_weight_basis: float32 [64, 1024], P(None, 'graph')
The draws below stay inside these ranges and needn't reach their ends.
Inputs may be any that keep to these rules, and one draw needn't show every extreme that they name: `edge_source`: the source atom of an edge may be any atom of its graph batch. `edge_target`: the target atom of an edge belongs to the edge's own device (edges g * 512 onward, atoms g * 8 onward). `trip_in`: every triplet slot of device g names an edge of device g. `trip_out`: every triplet slot of device g names an edge of device g. `block_counts`: in every batch some device uses all 8 blocks.
All inputs are finite; a program needn't handle non-finite values.
Results may differ from the reference program's by a relative error of at most 0.0074.
Values may be sent and summed in bfloat16 or wider, within the bound.
A program may use at most 32 MiB of HBM per device.

```python
import jax
import jax.numpy as jnp
from jax import lax

D = 1024
NB = 64
BLOCK = 128
E_DEV = 512
A_DEV = 8
TB_DEV = 8
ATOMS = 256
EDGES = 16384
TRIP_DEV = 1024
TRIPLETS = 32768
N_DP = 24
N_GRAPH = 32


def draw_edge_source(key, part):
    key = jax.random.fold_in(key, 1)
    return jax.random.randint(key, (N_DP, EDGES), 0, ATOMS).astype(jnp.int32)


def draw_edge_target(key, part):
    key = jax.random.fold_in(key, 2)
    within = jax.random.randint(key, (N_DP, EDGES), 0, A_DEV)
    device = jnp.arange(EDGES, dtype=jnp.int32) // E_DEV
    return (device[None, :] * A_DEV + within).astype(jnp.int32)


def edge_slots(key):
    within = jax.random.randint(key, (N_DP, TRIPLETS), 0, E_DEV)
    device = jnp.arange(TRIPLETS, dtype=jnp.int32) // TRIP_DEV
    return (device[None, :] * E_DEV + within).astype(jnp.int32)


def draw_trip_in(key, part):
    key = jax.random.fold_in(key, 3)
    return edge_slots(key)


def draw_trip_out(key, part):
    key = jax.random.fold_in(key, 4)
    return edge_slots(key)


def draw_block_counts(key, part):
    key = jax.random.fold_in(key, 5)
    first, second = jax.random.split(key)
    counts = jax.random.randint(first, (N_DP, N_GRAPH), max(1, TB_DEV // 4), TB_DEV + 1)
    chosen = jax.random.randint(second, (N_DP, 1), 0, N_GRAPH)
    column = jnp.arange(N_GRAPH, dtype=jnp.int32)[None, :]
    return jnp.where(column == chosen, TB_DEV, counts).astype(jnp.int32)


def level_of(own_key, extent, cuts, smallest, largest):
    loudness, own = 1.0, jax.random.fold_in(own_key, 6)
    for axis_at, shards_of in cuts:
        steps = jnp.exp(jax.random.uniform(jax.random.fold_in(own, axis_at), (shards_of,), jnp.float32, smallest / len(cuts), largest / len(cuts)))
        loudness = loudness * jnp.repeat(steps, extent[axis_at] // shards_of).reshape([-1 if axis == axis_at else 1 for axis in range(len(extent))])
    return loudness


def bell_draw(own_key, dims, width, limit, shards=(), kind=jnp.bfloat16):
    level = level_of(own_key, dims, shards, -0.22, 0.18) if shards else 1.0
    entries = jax.random.normal(own_key, dims, jnp.float32) * width * level
    return jnp.minimum(jnp.maximum(entries, -limit), limit).astype(kind)


def setup_inputs(seed: int = 0) -> dict:
    streams_of = jax.random.split(jax.random.key(seed), 12)
    atom_h = bell_draw(streams_of[0], (N_DP, ATOMS, D), 1.0, 6.0, ((0, 24), (1, 32)))
    edge_x = bell_draw(streams_of[1], (N_DP, EDGES, D), 1.0, 6.0, ((0, 24), (1, 32)))
    edge_source = draw_edge_source(jax.random.fold_in(streams_of[11], 71), 0)
    edge_target = draw_edge_target(jax.random.fold_in(streams_of[11], 71), 0)
    trip_in = draw_trip_in(jax.random.fold_in(streams_of[11], 71), 0)
    trip_out = draw_trip_out(jax.random.fold_in(streams_of[11], 71), 0)
    basis = bell_draw(streams_of[6], (N_DP, NB, TRIPLETS), 1.0, 6.0, ((0, 24), (2, 32)))
    block_counts = draw_block_counts(jax.random.fold_in(streams_of[11], 71), 0)
    atom_cotangent = bell_draw(streams_of[8], (N_DP, ATOMS, D), 1.0, 6.0, ((0, 24), (1, 32)))
    weight_edge = bell_draw(streams_of[9], (D, D), D ** -0.5, 0.1875)
    weight_basis = bell_draw(streams_of[10], (NB, D), NB ** -0.5, 0.75)
    return {"atom_h": atom_h, "edge_x": edge_x, "edge_source": edge_source, "edge_target": edge_target, "trip_in": trip_in, "trip_out": trip_out, "basis": basis, "block_counts": block_counts, "atom_cotangent": atom_cotangent, "weight_edge": weight_edge, "weight_basis": weight_basis}


def silu_slope(pre):
    logistic = jax.nn.sigmoid(pre)
    return logistic * (1.0 + pre * (1.0 - logistic))


def reference(atom_h, edge_x, edge_source, edge_target, trip_in, trip_out, basis, block_counts, atom_cotangent, weight_edge, weight_basis):
    slots = jnp.arange(TRIPLETS, dtype=jnp.int32)
    owner = slots // TRIP_DEV
    block_id = (slots % TRIP_DEV) // BLOCK

    def one_batch(items):
        hrows, xrows, source, target, tin, tout, bas, counts, cotan = items
        used = (block_id < counts[owner])[:, None]
        joined = (xrows.astype(jnp.float32) + hrows[source].astype(jnp.float32) + hrows[target].astype(jnp.float32)).astype(jnp.bfloat16)
        pre = jnp.dot(joined, weight_edge, preferred_element_type=jnp.float32)
        message = jax.nn.silu(pre).astype(jnp.bfloat16)
        spread = jnp.dot(bas.T, weight_basis, preferred_element_type=jnp.float32).astype(jnp.bfloat16)
        edge_grad = cotan[target]
        out_grad = edge_grad[tout].astype(jnp.float32)
        grad_msg = jnp.where(used, spread.astype(jnp.float32) * out_grad, 0.0).astype(jnp.bfloat16)
        grad_spread = jnp.where(used, message[tin].astype(jnp.float32) * out_grad, 0.0).astype(jnp.bfloat16)
        grad_message = jax.ops.segment_sum(grad_msg.astype(jnp.float32), tin, num_segments=EDGES)
        grad_wb = jnp.dot(bas, grad_spread, preferred_element_type=jnp.float32)
        grad_pre = (grad_message * silu_slope(pre)).astype(jnp.bfloat16)
        grad_w = jnp.dot(joined.T, grad_pre, preferred_element_type=jnp.float32)
        grad_x = jnp.dot(grad_pre, weight_edge.T, preferred_element_type=jnp.float32).astype(jnp.bfloat16)
        gxf = grad_x.astype(jnp.float32)
        grad_h = (cotan.astype(jnp.float32) + jax.ops.segment_sum(gxf, source, num_segments=ATOMS) + jax.ops.segment_sum(gxf, target, num_segments=ATOMS)).astype(jnp.bfloat16)
        return grad_x, grad_h, grad_w, grad_wb

    grad_x, grad_h, grad_w, grad_wb = lax.map(one_batch, (atom_h, edge_x, edge_source, edge_target, trip_in, trip_out, basis, block_counts, atom_cotangent))
    return grad_x, grad_h, jnp.sum(grad_w, axis=0), jnp.sum(grad_wb, axis=0)
```

```python
import jax
import jax.numpy as jnp
from jax import lax
from jax.experimental import pallas as pl
from jax.experimental.pallas import tpu as pltpu
from jax.sharding import PartitionSpec as P

BLOCK = 128
NX, NY, NC = 2, 8, 2
MESH = pl.DeviceIdType.MESH
F32 = jnp.float32
BF16 = jnp.bfloat16
TN = (((0,), (0,)), ((), ()))
NT = (((1,), (1,)), ((), ()))
DIST = (4, 3, 3, 2, 2, 1, 1)
HALF = (0, 1, 0, 1, 0, 1, 0)
ORDER = (4, 3, 5, 2, 6, 1, 7, 0)


def dot(a, b, dims=None):
    if dims is None:
        return jnp.dot(a, b, preferred_element_type=F32)
    return lax.dot_general(a, b, dims, preferred_element_type=F32)


def kernel(
    n_dp,
    h_ref,
    x_hbm,
    src_ref,
    tgt_ref,
    tin_ref,
    tout_ref,
    basis_ref,
    counts_ref,
    cot_ref,
    we_hbm,
    wb_ref,
    gx_hbm,
    gh_ref,
    gw_ref,
    gwb_ref,
    x_ref,
    we_ref,
    table,
    tab,
    mt_ref,
    g_ref,
    gm_ref,
    joined_ref,
    gp_ref,
    gx_ref,
    part,
    from_core,
    from_left,
    from_right,
    acc,
    x_out,
    x_in,
    dp_out,
    dp_in,
    dp_all,
    load_sem,
    ag_send,
    ag_recv,
    sib_send,
    sib_recv,
    core_send,
    core_recv,
    left_send,
    left_recv,
    right_send,
    right_recv,
    pair_send,
    pair_recv,
    dps_send,
    dps_recv,
    dpg_send,
    dpg_recv,
):
    edges, width = x_ref.shape
    nb, trips = basis_ref.shape
    atoms_dev = h_ref.shape[0]
    half = width // 2
    wcols = 2 * width
    bcols = wcols + 128
    cols = bcols + half
    blocks = bcols // 128
    chips = NX * NY
    dp = lax.axis_index("dp")
    g = lax.axis_index("graph")
    chip = lax.div(g, NC)
    c = lax.rem(g, NC)
    xl = lax.div(chip, NY)
    y = lax.rem(chip, NY)
    oc = 1 - c
    sibling = {"graph": chip * NC + oc}
    right = {"graph": (xl * NY + lax.rem(y + 1, NY)) * NC + c}
    left = {"graph": (xl * NY + lax.rem(y + NY - 1, NY)) * NC + c}
    across = {"graph": ((1 - xl) * NY + y) * NC + c}

    def chip_peer(k):
        return lax.rem(chip + k, chips)

    def signal(sem, device):
        pl.semaphore_signal(sem, inc=1, device_id=device, device_id_type=MESH)

    def remote(src, dst, send, recv, device):
        return pltpu.make_async_remote_copy(
            src_ref=src,
            dst_ref=dst,
            send_sem=send,
            recv_sem=recv,
            device_id=device,
            device_id_type=MESH,
        )

    barrier = pltpu.get_barrier_semaphore()
    signal(barrier, sibling)

    @pl.loop(1, chips)
    def _(k):
        signal(barrier, {"graph": chip_peer(k) * NC + c})

    @pl.loop(1, n_dp)
    def _(k):
        signal(barrier, {"dp": lax.rem(dp + k, n_dp)})

    load_x = pltpu.make_async_copy(x_hbm, x_ref, load_sem.at[0])
    load_x.start()
    load_we = pltpu.make_async_copy(we_hbm, we_ref, load_sem.at[1])
    load_we.start()

    hrows = h_ref[...].astype(F32)
    own_rows = jnp.concatenate([hrows[:, :half], hrows[:, half:]], axis=0).astype(BF16)
    table[chip, c] = own_rows
    pl.semaphore_wait(barrier, chips + n_dp - 1)

    def table_copy(k):
        return remote(
            table.at[chip, c],
            table.at[chip, c],
            ag_send.at[k],
            ag_recv.at[chip],
            {"graph": chip_peer(k) * NC + c},
        )

    def table_arrival(k):
        s = chip_peer(k)
        return remote(
            table.at[s, c], table.at[s, c], ag_send.at[k], ag_recv.at[s], sibling
        )

    def forward(k):
        s = chip_peer(k)
        return remote(
            table.at[s, c], table.at[s, c], sib_send.at[s], sib_recv.at[s], sibling
        )

    def forward_arrival(k):
        s = chip_peer(k)
        return remote(
            table.at[s, oc], table.at[s, oc], sib_send.at[s], sib_recv.at[s], sibling
        )

    @pl.loop(1, chips)
    def _(k):
        table_copy(k).start()

    forward(0).start()

    edge_of_slot = lax.broadcasted_iota(jnp.int32, (edges, trips), 0)
    edge_base = g * edges
    atom_base = g * atoms_dev
    hits_out = (edge_of_slot == tout_ref[...] - edge_base).astype(F32).astype(BF16)
    target_hits = (
        (lax.broadcasted_iota(jnp.int32, (16, edges), 0) == tgt_ref[...] - atom_base)
        .astype(F32)
        .astype(BF16)
    )
    a_of = dot(target_hits, hits_out)
    slot = lax.broadcasted_iota(jnp.int32, (1, trips), 1)
    a_of = jnp.where(slot < counts_ref[0, 0] * BLOCK, a_of, 0.0)
    hits_in = (edge_of_slot == tin_ref[...] - edge_base).astype(F32).astype(BF16)
    basis = basis_ref[...].astype(F32)
    group = 256 // nb
    for q in range(atoms_dev // group):
        spreadout = jnp.concatenate(
            [basis * a_of[a : a + 1, :] for a in range(q * group, (q + 1) * group)], axis=0
        ).astype(BF16)
        mt_ref[:, q * 256 : (q + 1) * 256] = dot(hits_in, spreadout, NT).astype(BF16)
    cot = cot_ref[...].astype(F32)
    wb = wb_ref[...].astype(F32)
    for a in range(atoms_dev):
        g_ref[a * nb : (a + 1) * nb, :] = (wb * cot[a : a + 1, :]).astype(BF16)
    for j in range(width // 256):
        js = slice(j * 256, (j + 1) * 256)
        gm_ref[:, js] = dot(mt_ref[...], g_ref[:, js])

    @pl.loop(1, chips)
    def _(k):
        table_arrival(k).wait_recv()
        forward(k).start()

    @pl.loop(0, chips)
    def _(k):
        forward_arrival(k).wait_recv()

    packed = table[...].astype(F32).reshape(chips * NC, 2 * atoms_dev, half)
    tab[:, :half] = packed[:, :atoms_dev, :].reshape(chips * NC * atoms_dev, half).astype(BF16)
    tab[:, half:] = packed[:, atoms_dev:, :].reshape(chips * NC * atoms_dev, half).astype(BF16)

    atom_of_edge = lax.broadcasted_iota(jnp.int32, (tab.shape[0], edges), 0)
    hits = (
        (atom_of_edge == src_ref[...]).astype(F32) + (atom_of_edge == tgt_ref[...]).astype(F32)
    ).astype(BF16)
    load_x.wait()
    for j in range(width // 256):
        js = slice(j * 256, (j + 1) * 256)
        ends = dot(hits, tab[:, js], TN)
        joined_ref[:, js] = (x_ref[:, js].astype(F32) + ends).astype(BF16)
    load_we.wait()

    def owner_of(number):
        return (number // NC) % NY, number // (NC * NY), number % NC

    for j in range(width // 256):
        js = slice(j * 256, (j + 1) * 256)
        pre = dot(joined_ref[...], we_ref[:, js])
        logistic = 1.0 / (1.0 + jnp.exp(-pre))
        message = (pre * logistic).astype(BF16)
        slope = logistic * (1.0 + pre * (1.0 - logistic))
        gp_ref[:, js] = (gm_ref[:, js] * slope).astype(BF16)
        spread_sum = dot(mt_ref[...], message, TN)
        gwb = jnp.zeros((nb, 256), F32)
        for a in range(atoms_dev):
            gwb = gwb + spread_sum[a * nb : (a + 1) * nb, :] * cot[a : a + 1, js]
        both = jnp.concatenate([gwb, pltpu.roll(gwb, 256 - 16, 1)], axis=0)
        turned = both.T.astype(BF16).reshape(8, 2, 16, 128)
        for k in range(8):
            py, px, pc = owner_of(j * 8 + k)
            part[py, px, pc, :, wcols:bcols] = turned[k, 0]
    for i in range(width // 256):
        gw = dot(joined_ref[:, i * 256 : (i + 1) * 256], gp_ref[...], TN).astype(BF16)
        for k in range(8):
            py, px, pc = owner_of(i * 8 + k)
            part[py, px, pc, :, :width] = gw[k * 32 : k * 32 + 16]
            part[py, px, pc, :, width:wcols] = gw[k * 32 + 16 : k * 32 + 32]

    for j in range(width // 256):
        js = slice(j * 256, (j + 1) * 256)
        gx_ref[:, js] = dot(gp_ref[...], we_ref[js, :], NT).astype(BF16)
    store_gx = pltpu.make_async_copy(gx_ref, gx_hbm, load_sem.at[2])
    store_gx.start()
    lo = dot(hits, gx_ref[:, :half])
    hi = dot(hits, gx_ref[:, half:])
    for number in range(chips * NC):
        py, px, pc = owner_of(number)
        rows = slice(number * atoms_dev, (number + 1) * atoms_dev)
        part[py, px, pc, :, bcols:] = jnp.concatenate([lo[rows], hi[rows]], axis=0).astype(BF16)

    core_copies = []
    for i, away in enumerate(ORDER):
        there = lax.rem(y + away, NY)
        copy = remote(
            part.at[there, :, oc], from_core.at[i], core_send.at[i], core_recv.at[i], sibling
        )
        copy.start()
        core_copies.append(copy)

    def add_core(i):
        core_copies[i].wait_recv()
        there = lax.rem(y + ORDER[i], NY)
        for px in range(NX):
            part[there, px, c] = (
                part[there, px, c].astype(F32) + from_core[i, px].astype(F32)
            ).astype(BF16)

    to_right, to_left = [], []
    for k, (dist, side) in enumerate(zip(DIST, HALF)):
        if k == 0:
            add_core(0)
        elif k % 2:
            add_core(k)
            add_core(k + 1)
        there = lax.rem(y + dist, NY)
        if k >= 2:
            to_right[k - 2].wait_recv()
            part[there, side, c] = (
                part[there, side, c].astype(F32) + from_left[k - 2].astype(F32)
            ).astype(BF16)
        copy = remote(
            part.at[there, side, c],
            from_left.at[k],
            right_send.at[k],
            right_recv.at[k],
            right,
        )
        copy.start()
        to_right.append(copy)
        there = lax.rem(y + NY - dist, NY)
        if k >= 2:
            to_left[k - 2].wait_recv()
            part[there, 1 - side, c] = (
                part[there, 1 - side, c].astype(F32) + from_right[k - 2].astype(F32)
            ).astype(BF16)
        copy = remote(
            part.at[there, 1 - side, c],
            from_right.at[k],
            left_send.at[k],
            left_recv.at[k],
            left,
        )
        copy.start()
        to_left.append(copy)
    core_copies[7].wait_recv()
    for k in (5, 6):
        to_right[k].wait_recv()
        to_left[k].wait_recv()
    last = len(DIST) - 1
    for px in range(NX):
        acc[px] = (
            part[y, px, c].astype(F32)
            + from_core[7, px].astype(F32)
            + from_left[last - px].astype(F32)
            + from_right[last - 1 + px].astype(F32)
        )

    x_out[...] = acc[1 - xl].astype(BF16)
    pair = remote(x_out, x_in, pair_send, pair_recv, across)
    pair.start()
    pair.wait_recv()
    total = acc[xl] + x_in[...].astype(F32)

    for b in range(blocks):
        dp_out[b] = total[:, b * 128 : (b + 1) * 128].astype(BF16)

    def share(d):
        return remote(
            dp_out.at[d], dp_in.at[dp], dps_send.at[d], dps_recv.at[dp], {"dp": d}
        )

    def share_arrival(s):
        return remote(
            dp_out.at[0], dp_in.at[s], dps_send.at[0], dps_recv.at[s], {"dp": s}
        )

    @pl.loop(0, blocks)
    def _(d):
        @pl.when(d != dp)
        def _():
            share(d).start()

    grad_h = total[:, bcols:]
    gh_ref[...] = (
        cot + jnp.concatenate([grad_h[:atoms_dev], grad_h[atoms_dev:]], axis=1)
    ).astype(BF16)

    def spread_total(k):
        d = lax.rem(dp + k, n_dp)
        return remote(
            dp_all.at[dp], dp_all.at[dp], dpg_send.at[k], dpg_recv.at[dp], {"dp": d}
        )

    @pl.when(dp < blocks)
    def _():
        dp_in[dp] = dp_out[dp]

        @pl.loop(1, n_dp)
        def _(k):
            share_arrival(lax.rem(dp + k, n_dp)).wait_recv()

        dp_all[dp] = jnp.sum(dp_in[...].astype(F32), axis=0)

        @pl.loop(1, n_dp)
        def _(k):
            spread_total(k).start()

    @pl.loop(0, blocks)
    def _(s):
        @pl.when(s != dp)
        def _():
            remote(
                dp_all.at[s], dp_all.at[s], dpg_send.at[0], dpg_recv.at[s], {"dp": s}
            ).wait_recv()

    per_row = width // 128
    for b in range(blocks - 1):
        r, q = b // per_row, b % per_row
        gw_ref[r * 16 : (r + 1) * 16, q * 128 : (q + 1) * 128] = dp_all[b]
    gwb_ref[...] = dp_all[blocks - 1]

    @pl.when(dp < blocks)
    def _():
        @pl.loop(1, n_dp)
        def _(k):
            spread_total(k).wait_send()

    @pl.loop(0, blocks)
    def _(d):
        @pl.when(d != dp)
        def _():
            share(d).wait_send()

    pair.wait_send()
    for copy in core_copies + to_right + to_left:
        copy.wait_send()

    @pl.loop(1, chips)
    def _(k):
        table_copy(k).wait_send()

    @pl.loop(0, chips)
    def _(k):
        forward(k).wait_send()

    store_gx.wait()


def shards(
    atom_h,
    edge_x,
    edge_source,
    edge_target,
    trip_in,
    trip_out,
    basis,
    block_counts,
    atom_cotangent,
    weight_edge,
    weight_basis,
):
    n_dp = lax.axis_size("dp")
    edges, width = edge_x.shape[1:]
    nb, trips = basis.shape[1:]
    atoms_dev = atom_h.shape[1]
    chips = NX * NY
    half = width // 2
    cols = 2 * width + 128 + half
    blocks = (2 * width + 128) // 128
    steps = len(DIST)
    vmem = pl.BlockSpec(memory_space=pltpu.VMEM)
    hbm = pl.BlockSpec(memory_space=pl.ANY)
    smem = pl.BlockSpec(memory_space=pltpu.SMEM)
    dma = pltpu.SemaphoreType.DMA
    grad_x, grad_h, grad_w, grad_wb = pl.pallas_call(
        lambda *refs: kernel(n_dp, *refs),
        out_shape=(
            jax.ShapeDtypeStruct((edges, width), BF16),
            jax.ShapeDtypeStruct((atoms_dev, width), BF16),
            jax.ShapeDtypeStruct((width // (chips * NC), width), F32),
            jax.ShapeDtypeStruct((16, 128), F32),
        ),
        in_specs=[vmem, hbm, vmem, vmem, vmem, vmem, vmem, smem, vmem, hbm, vmem],
        out_specs=(hbm, vmem, vmem, vmem),
        scratch_shapes=[
            pltpu.VMEM((edges, width), BF16),
            pltpu.VMEM((width, width), BF16),
            pltpu.VMEM((chips, NC, 2 * atoms_dev, half), BF16),
            pltpu.VMEM((chips * NC * atoms_dev, width), BF16),
            pltpu.VMEM((edges, atoms_dev * nb), BF16),
            pltpu.VMEM((atoms_dev * nb, width), BF16),
            pltpu.VMEM((edges, width), F32),
            pltpu.VMEM((edges, width), BF16),
            pltpu.VMEM((edges, width), BF16),
            pltpu.VMEM((edges, width), BF16),
            pltpu.VMEM((NY, NX, NC, 16, cols), BF16),
            pltpu.VMEM((NY, NX, 16, cols), BF16),
            pltpu.VMEM((steps, 16, cols), BF16),
            pltpu.VMEM((steps, 16, cols), BF16),
            pltpu.VMEM((NX, 16, cols), F32),
            pltpu.VMEM((16, cols), BF16),
            pltpu.VMEM((16, cols), BF16),
            pltpu.VMEM((blocks, 16, 128), BF16),
            pltpu.VMEM((n_dp, 16, 128), BF16),
            pltpu.VMEM((blocks, 16, 128), F32),
            dma((3,)),
            dma((chips,)),
            dma((chips,)),
            dma((chips,)),
            dma((chips,)),
            dma((NY,)),
            dma((NY,)),
            dma((steps,)),
            dma((steps,)),
            dma((steps,)),
            dma((steps,)),
            dma,
            dma,
            dma((blocks,)),
            dma((n_dp,)),
            dma((n_dp,)),
            dma((n_dp,)),
        ],
        compiler_params=pltpu.CompilerParams(
            collective_id=0, has_side_effects=True, vmem_limit_bytes=48 * 1024 * 1024
        ),
    )(
        atom_h[0],
        edge_x[0],
        edge_source,
        edge_target,
        trip_in,
        trip_out,
        basis[0],
        block_counts,
        atom_cotangent[0],
        weight_edge,
        weight_basis,
    )
    turned = grad_wb.T
    grad_wb = jnp.concatenate([turned[:nb], turned[nb:]], axis=1)
    return (grad_x[None], grad_h[None], grad_w, grad_wb)


def solution(mesh):
    placed = (
        P("dp", "graph", None),
        P("dp", "graph", None),
        P("dp", "graph"),
        P("dp", "graph"),
        P("dp", "graph"),
        P("dp", "graph"),
        P("dp", None, "graph"),
        P("dp", "graph"),
        P("dp", "graph", None),
        P(),
        P(),
    )
    return jax.shard_map(
        shards,
        mesh=mesh,
        in_specs=placed,
        out_specs=(
            P("dp", "graph", None),
            P("dp", "graph", None),
            P("graph", None),
            P(None, "graph"),
        ),
        check_vma=False,
    )
```

```python
import jax
import jax.numpy as jnp
from jax import lax
from jax.experimental import pallas as pl
from jax.experimental.pallas import tpu as pltpu
from jax.sharding import PartitionSpec as P

BLOCK = 128
NX, NY, NC = 2, 8, 2
MESH = pl.DeviceIdType.MESH
F32 = jnp.float32
BF16 = jnp.bfloat16
TN = (((0,), (0,)), ((), ()))
NT = (((1,), (1,)), ((), ()))
DIST = (4, 3, 3, 2, 2, 1, 1)
HALF = (0, 1, 0, 1, 0, 1, 0)
PLACES = (0, -1, -2, 1, 2, -3, 3, 4)


def dot(a, b, dims=None):
    if dims is None:
        return jnp.dot(a, b, preferred_element_type=F32)
    return lax.dot_general(a, b, dims, preferred_element_type=F32)


def kernel(
    n_dp,
    h_hbm,
    x_hbm,
    src_hbm,
    tgt_hbm,
    tin_hbm,
    tout_hbm,
    basis_hbm,
    counts_hbm,
    cot_hbm,
    we_hbm,
    wb_hbm,
    gx_hbm,
    gh_ref,
    gw_ref,
    gwb_ref,
    h_ref,
    x_ref,
    src_ref,
    tgt_ref,
    tin_ref,
    tout_ref,
    basis_ref,
    counts_ref,
    cot_ref,
    we_ref,
    wb_ref,
    table,
    tab,
    mt_ref,
    g_ref,
    gm_ref,
    joined_ref,
    gp_ref,
    gx_ref,
    msg_ref,
    part_w,
    part_s,
    core_w,
    core_s,
    left_w,
    left_s,
    right_w,
    right_s,
    acc_w,
    acc_s,
    x_out_w,
    x_in_w,
    x_out_b,
    x_in_b,
    x_out_h,
    x_in_h,
    dp_out,
    dp_in,
    dp_all,
    load_sem,
    tab_send,
    tab_recv,
    tabx_send,
    tabx_recv,
    sib_send,
    sib_recv,
    core_send,
    core_recv,
    left_send,
    left_recv,
    right_send,
    right_recv,
    x_send,
    x_recv,
    dps_send,
    dps_recv,
    dpg_send,
    dpg_recv,
):
    edges, width = x_ref.shape
    nb, trips = basis_ref.shape
    atoms_dev = h_ref.shape[0]
    half = width // 2
    tiles = width // 128
    nz = n_dp // 2
    dp = lax.axis_index("dp")
    g = lax.axis_index("graph")
    chip = lax.div(g, NC)
    c = lax.rem(g, NC)
    xl = lax.div(chip, NY)
    y = lax.rem(chip, NY)
    oc = 1 - c
    xh = lax.div(dp, nz)
    z = lax.rem(dp, nz)

    def along(offset):
        return lax.rem(y + (offset + NY), NY)

    def y_peer(offset):
        return {"graph": (xl * NY + along(offset)) * NC + c}

    sibling = {"graph": chip * NC + oc}
    right, left = y_peer(1), y_peer(-1)
    other_graph = ((1 - xl) * NY + y) * NC + c
    other_dp = (1 - xh) * nz + z
    across = {"graph": other_graph}
    x_peers = (across, {"dp": other_dp}, {"dp": other_dp, "graph": other_graph})

    def signal(sem, device):
        pl.semaphore_signal(sem, inc=1, device_id=device, device_id_type=MESH)

    def remote(src, dst, send, recv, device):
        return pltpu.make_async_remote_copy(
            src_ref=src,
            dst_ref=dst,
            send_sem=send,
            recv_sem=recv,
            device_id=device,
            device_id_type=MESH,
        )

    sent = []

    def begin(copy):
        copy.start()
        sent.append(copy)

    loads = [
        pltpu.make_async_copy(src, dst, load_sem.at[i])
        for i, (src, dst) in enumerate(
            [
                (h_hbm, h_ref),
                (tout_hbm, tout_ref),
                (tgt_hbm, tgt_ref),
                (tin_hbm, tin_ref),
                (counts_hbm, counts_ref),
                (basis_hbm, basis_ref),
                (wb_hbm, wb_ref),
                (cot_hbm, cot_ref),
                (src_hbm, src_ref),
                (x_hbm, x_ref),
                (we_hbm, we_ref),
            ]
        )
    ]
    for load in loads:
        load.start()
    load_h, load_x, load_we = loads[0], loads[-2], loads[-1]

    barrier = pltpu.get_barrier_semaphore()
    greeted = [sibling, right, left, y_peer(2), y_peer(-2), across, x_peers[2]]
    for peer in greeted:
        signal(barrier, peer)

    @pl.loop(1, n_dp)
    def _(k):
        signal(barrier, {"dp": lax.rem(dp + k, n_dp)})

    load_h.wait()
    hrows = h_ref[...].astype(F32)
    own_rows = jnp.concatenate([hrows[:, :half], hrows[:, half:]], axis=0).astype(BF16)
    table[xl, y, c] = own_rows
    pl.semaphore_wait(barrier, len(greeted) + n_dp - 1)

    def block(offset, part=None):
        if part is None:
            return table.at[xl, along(offset), c]
        return table.at[xl, along(offset), c, :, part * (half // 2) : (part + 1) * (half // 2)]

    number = {-1: 0, -2: 1, 1: 2, 2: 3, -3: 4, 3: 5, -4: 6, 4: 7}
    side = {-4: 0, 4: 1}

    def table_send(offset, to):
        seen = offset - to
        i, ref = number[seen], block(offset, side.get(seen))
        begin(remote(ref, ref, tab_send.at[i], tab_recv.at[i], y_peer(to)))

    def table_wait(seen):
        i, ref = number[seen], block(seen, side.get(seen))
        remote(ref, ref, tab_send.at[i], tab_recv.at[i], sibling).wait_recv()

    def across_send(i):
        ref = block(PLACES[i])
        begin(remote(ref, ref, tabx_send.at[i], tabx_recv.at[i], across))

    def across_wait(i):
        ref = table.at[1 - xl, along(PLACES[i]), c]
        remote(ref, ref, tabx_send.at[i], tabx_recv.at[i], sibling).wait_recv()

    def sibling_send(i, other):
        ref = table.at[(1 - xl) if other else xl, along(PLACES[i]), c]
        j = other * NY + i
        begin(remote(ref, ref, sib_send.at[j], sib_recv.at[j], sibling))

    def sibling_wait(i, other):
        ref = table.at[(1 - xl) if other else xl, along(PLACES[i]), oc]
        j = other * NY + i
        remote(ref, ref, sib_send.at[j], sib_recv.at[j], sibling).wait_recv()

    for to in (2, -2, 1, -1):
        table_send(0, to)
    across_send(0)
    sibling_send(0, 0)

    for load in loads[1:-2]:
        load.wait()
    edge_of_slot = lax.broadcasted_iota(jnp.int32, (edges, trips), 0)
    edge_base = g * edges
    atom_base = g * atoms_dev
    hits_out = (edge_of_slot == tout_ref[...] - edge_base).astype(F32).astype(BF16)
    target_hits = (
        (lax.broadcasted_iota(jnp.int32, (16, edges), 0) == tgt_ref[...] - atom_base)
        .astype(F32)
        .astype(BF16)
    )
    a_of = dot(target_hits, hits_out)
    slot = lax.broadcasted_iota(jnp.int32, (1, trips), 1)
    a_of = jnp.where(slot < counts_ref[0, 0] * BLOCK, a_of, 0.0)

    for seen, to in ((-2, 1), (2, -1), (-2, 2), (2, -2)):
        if abs(to) == 1:
            table_wait(seen)
        table_send(seen, to)
    table_wait(-1)
    table_wait(1)
    for i in (2, 4, 1, 3):
        across_send(i)
    for i in (2, 4, 1, 3):
        sibling_send(i, 0)

    hits_in = (edge_of_slot == tin_ref[...] - edge_base).astype(F32).astype(BF16)
    basis = basis_ref[...].astype(F32)
    group = 256 // nb
    for q in range(atoms_dev // group):
        spreadout = jnp.concatenate(
            [basis * a_of[a : a + 1, :] for a in range(q * group, (q + 1) * group)], axis=0
        ).astype(BF16)
        mt_ref[:, q * 256 : (q + 1) * 256] = dot(hits_in, spreadout, NT).astype(BF16)

    for seen in (-3, 3, -4, 4):
        table_wait(seen)
    for i in (5, 6, 7):
        across_send(i)
    for i in (5, 6, 7):
        sibling_send(i, 0)
    for i in (0, 2, 4, 1, 3):
        across_wait(i)
        sibling_send(i, 1)

    cot = cot_ref[...].astype(F32)
    wb = wb_ref[...].astype(F32)
    for a in range(atoms_dev):
        g_ref[a * nb : (a + 1) * nb, :] = (wb * cot[a : a + 1, :]).astype(BF16)
    for j in range(width // 256):
        js = slice(j * 256, (j + 1) * 256)
        gm_ref[:, js] = dot(mt_ref[...], g_ref[:, js])

    for i in (5, 6, 7):
        across_wait(i)
        sibling_send(i, 1)
    for i in range(NY):
        sibling_wait(i, 0)
        sibling_wait(i, 1)

    all_atoms = NX * NY * NC * atoms_dev
    packed = table[...].astype(F32).reshape(NX * NY * NC, 2 * atoms_dev, half)
    tab[:, :half] = packed[:, :atoms_dev, :].reshape(all_atoms, half).astype(BF16)
    tab[:, half:] = packed[:, atoms_dev:, :].reshape(all_atoms, half).astype(BF16)

    atom_of_edge = lax.broadcasted_iota(jnp.int32, (all_atoms, edges), 0)
    hits = (
        (atom_of_edge == src_ref[...]).astype(F32) + (atom_of_edge == tgt_ref[...]).astype(F32)
    ).astype(BF16)
    load_x.wait()
    for j in range(width // 256):
        js = slice(j * 256, (j + 1) * 256)
        ends = dot(hits, tab[:, js], TN)
        joined_ref[:, js] = (x_ref[:, js].astype(F32) + ends).astype(BF16)
    load_we.wait()
    for j in range(width // 256):
        js = slice(j * 256, (j + 1) * 256)
        pre = dot(joined_ref[...], we_ref[:, js])
        logistic = 1.0 / (1.0 + jnp.exp(-pre))
        msg_ref[:, js] = (pre * logistic).astype(BF16)
        slope = logistic * (1.0 + pre * (1.0 - logistic))
        gp_ref[:, js] = (gm_ref[:, js] * slope).astype(BF16)

    def core_copy(part, landing, sem, there):
        return remote(
            part.at[there, :, oc],
            landing.at[there],
            core_send.at[sem, there],
            core_recv.at[sem, there],
            sibling,
        )

    near = lax.div(y, 4)
    for far in (1 - near, near):
        for px in range(NX):
            rows = pl.ds(pl.multiple_of((px * 2 + far) * 256, 256), 256)
            gw = dot(joined_ref[:, rows], gp_ref[...], TN).astype(BF16)
            for k in range(8):
                py = far * 4 + k // 2
                part_w[py, px, k % 2, :, :width] = gw[k * 32 : k * 32 + 16]
                part_w[py, px, k % 2, :, width:] = gw[k * 32 + 16 : k * 32 + 32]
        for m in range(4):
            begin(core_copy(part_w, core_w, 0, far * 4 + lax.rem(y + m, 4)))

    def stream(sem, part, landing, from_left, from_right):
        def add_core(offset):
            there = along(offset)
            core_copy(part, landing, sem, there).wait_recv()
            for px in range(NX):
                part[there, px, c] = (
                    part[there, px, c].astype(F32) + landing[there, px].astype(F32)
                ).astype(BF16)

        def copies(k):
            right_ref = part.at[along(DIST[k]), HALF[k], c]
            left_ref = part.at[along(-DIST[k]), 1 - HALF[k], c]
            return (
                remote(
                    right_ref, from_left.at[k], right_send.at[sem, k], right_recv.at[sem, k], right
                ),
                remote(
                    left_ref, from_right.at[k], left_send.at[sem, k], left_recv.at[sem, k], left
                ),
            )

        def step(k):
            if k == 0:
                add_core(4)
            elif k % 2:
                add_core(DIST[k])
                add_core(-DIST[k])
            to_right, to_left = copies(k)
            if k >= 2:
                before_right, before_left = copies(k - 2)
                there = along(DIST[k])
                before_right.wait_recv()
                part[there, HALF[k], c] = (
                    part[there, HALF[k], c].astype(F32) + from_left[k - 2].astype(F32)
                ).astype(BF16)
                begin(to_right)
                there = along(-DIST[k])
                before_left.wait_recv()
                part[there, 1 - HALF[k], c] = (
                    part[there, 1 - HALF[k], c].astype(F32) + from_right[k - 2].astype(F32)
                ).astype(BF16)
                begin(to_left)
            else:
                begin(to_right)
                begin(to_left)

        def finish():
            core_copy(part, landing, sem, y).wait_recv()
            for k in (5, 6):
                for copy in copies(k):
                    copy.wait_recv()
            return [
                part[y, px, c].astype(F32)
                + landing[y, px].astype(F32)
                + from_left[6 - px].astype(F32)
                + from_right[5 + px].astype(F32)
                for px in range(NX)
            ]

        return step, finish

    step_w, finish_w = stream(0, part_w, core_w, left_w, right_w)
    step_s, finish_s = stream(1, part_s, core_s, left_s, right_s)

    def owner_of(number):
        return (number // NC) % NY, number // (NC * NY), number % NC

    def basis_piece(j):
        js = slice(j * 256, (j + 1) * 256)
        spread_sum = dot(mt_ref[...], msg_ref[:, js], TN)
        gwb = jnp.zeros((nb, 256), F32)
        for a in range(atoms_dev):
            gwb = gwb + spread_sum[a * nb : (a + 1) * nb, :] * cot[a : a + 1, js]
        both = jnp.concatenate([gwb, pltpu.roll(gwb, 256 - 16, 1)], axis=0)
        turned = both.T.astype(BF16).reshape(8, 2, 16, 128)
        for k in range(8):
            py, px, pc = owner_of(j * 8 + k)
            part_s[py, px, pc, :, :128] = turned[k, 0]

    def grad_x_piece(j):
        js = slice(j * 256, (j + 1) * 256)
        gx_ref[:, js] = dot(gp_ref[...], we_ref[js, :], NT).astype(BF16)

    def atoms_piece():
        lo = dot(hits, gx_ref[:, :half])
        hi = dot(hits, gx_ref[:, half:])
        for number in range(NX * NY * NC):
            py, px, pc = owner_of(number)
            rows = slice(number * atoms_dev, (number + 1) * atoms_dev)
            part_s[py, px, pc, :, 128:] = jnp.concatenate([lo[rows], hi[rows]], axis=0).astype(
                BF16
            )

    step_w(0)
    step_w(1)
    grad_x_piece(0)
    grad_x_piece(1)
    step_w(2)
    grad_x_piece(2)
    grad_x_piece(3)
    step_w(3)
    store_gx = pltpu.make_async_copy(gx_ref, gx_hbm, load_sem.at[11])
    store_gx.start()
    basis_piece(0)
    basis_piece(1)
    step_w(4)
    basis_piece(2)
    basis_piece(3)
    step_w(5)
    atoms_piece()
    for m in (4, 3, 5, 2, 6, 1, 7, 0):
        begin(core_copy(part_s, core_s, 1, along(m - NY)))
    step_w(6)
    step_s(0)
    step_s(1)

    for px, value in enumerate(finish_w()):
        acc_w[px, 0] = value[:, :width]
        acc_w[px, 1] = value[:, width:]
    quarters = ((1 - xl, xh), (xl, 1 - xh), (1 - xl, 1 - xh))

    def x_copy(kind, p, out, landing):
        return remote(out, landing, x_send.at[kind, p], x_recv.at[kind, p], x_peers[p])

    def x_copy_w(p):
        return x_copy(0, p, x_out_w.at[p], x_in_w.at[p])

    def x_copy_b(p):
        return x_copy(1, p, x_out_b.at[p], x_in_b.at[p])

    x_copy_h = x_copy(2, 0, x_out_h, x_in_h)
    for p, (qx, qh) in enumerate(quarters):
        x_out_w[p] = acc_w[qx, qh].astype(BF16)
        begin(x_copy_w(p))
    for k in range(2, len(DIST)):
        step_s(k)
    for px, value in enumerate(finish_s()):
        acc_s[px] = value
    for p, (qx, qh) in enumerate(quarters):
        x_out_b[p] = acc_s[qx, :, :128].astype(BF16)
        begin(x_copy_b(p))
    x_out_h[...] = acc_s[1 - xl, :, 128:].astype(BF16)
    begin(x_copy_h)

    total_w = acc_w[xl, xh]
    total_b = acc_s[xl, :, :128]
    for p in range(3):
        x_copy_w(p).wait_recv()
        total_w = total_w + x_in_w[p].astype(F32)
    for p in range(3):
        x_copy_b(p).wait_recv()
        total_b = total_b + x_in_b[p].astype(F32)

    for t in range(tiles):
        dp_out[t] = total_w[:, t * 128 : (t + 1) * 128].astype(BF16)
    dp_out[tiles] = total_b.astype(BF16)
    mine = tiles + xh

    def share(t):
        return remote(
            dp_out.at[t], dp_in.at[z], dps_send.at[t], dps_recv.at[z], {"dp": xh * nz + t}
        )

    @pl.loop(0, mine)
    def _(t):
        @pl.when(t != z)
        def _():
            share(t).start()

    x_copy_h.wait_recv()
    grad_h = acc_s[xl, :, 128:] + x_in_h[...].astype(F32)
    gh_ref[...] = (
        cot + jnp.concatenate([grad_h[:atoms_dev], grad_h[atoms_dev:]], axis=1)
    ).astype(BF16)

    own_tile = xh * tiles + z

    def spread_total(k):
        return remote(
            dp_all.at[own_tile],
            dp_all.at[own_tile],
            dpg_send.at[k],
            dpg_recv.at[own_tile],
            {"dp": lax.rem(dp + k, n_dp)},
        )

    @pl.when(z < mine)
    def _():
        dp_in[z] = dp_out[z]

        @pl.loop(1, nz)
        def _(k):
            s = lax.rem(z + k, nz)
            remote(
                dp_out.at[0], dp_in.at[s], dps_send.at[0], dps_recv.at[s], sibling
            ).wait_recv()

        dp_all[own_tile] = jnp.sum(dp_in[...].astype(F32), axis=0).astype(BF16)

        @pl.loop(1, n_dp)
        def _(k):
            spread_total(k).start()

    @pl.loop(0, 2 * tiles + 1)
    def _(t):
        @pl.when(jnp.logical_or(t != own_tile, z >= mine))
        def _():
            remote(
                dp_all.at[t], dp_all.at[t], dpg_send.at[0], dpg_recv.at[t], sibling
            ).wait_recv()

    for t in range(2 * tiles):
        r, q = t // tiles, t % tiles
        gw_ref[r * 16 : (r + 1) * 16, q * 128 : (q + 1) * 128] = dp_all[t].astype(F32)
    gwb_ref[...] = dp_all[2 * tiles].astype(F32)

    @pl.when(z < mine)
    def _():
        @pl.loop(1, n_dp)
        def _(k):
            spread_total(k).wait_send()

    @pl.loop(0, mine)
    def _(t):
        @pl.when(t != z)
        def _():
            share(t).wait_send()

    for copy in sent:
        copy.wait_send()
    store_gx.wait()


def write_out(gx, gh, gw, gwb, gx_hbm, gh_hbm, gw_hbm, gwb_hbm, gx_ref, gh_ref, gw_ref, in_ref, out_ref, get, put):
    rows = gx_ref.shape[0] // 4
    nb = out_ref.shape[1]
    moves = [(gwb, in_ref, out_ref, gwb_hbm), (gh, gh_ref, gh_ref, gh_hbm), (gw, gw_ref, gw_ref, gw_hbm)]
    for i in range(4):
        part = pl.ds(i * rows, rows)
        moves.append((gx.at[part], gx_ref.at[part], gx_ref.at[part], gx_hbm.at[part]))
    gets = [pltpu.make_async_copy(a, b, get.at[i]) for i, (a, b, _, _) in enumerate(moves)]
    puts = [pltpu.make_async_copy(a, b, put.at[i]) for i, (_, _, a, b) in enumerate(moves)]
    for copy in gets:
        copy.start()
    for i, copy in enumerate(puts):
        gets[i].wait()
        if i == 0:
            out_ref[:16, :] = in_ref[:, :nb]
            out_ref[16:, :] = in_ref[:, nb:]
        copy.start()
    for copy in puts:
        copy.wait()


def shards(
    atom_h,
    edge_x,
    edge_source,
    edge_target,
    trip_in,
    trip_out,
    basis,
    block_counts,
    atom_cotangent,
    weight_edge,
    weight_basis,
):
    n_dp = lax.axis_size("dp")
    edges, width = edge_x.shape[1:]
    nb, trips = basis.shape[1:]
    atoms_dev = atom_h.shape[1]
    owned = width // (NX * NY * NC)
    half = width // 2
    small = 128 + half
    steps = len(DIST)
    tiles = width // 128
    vmem = pl.BlockSpec(memory_space=pltpu.VMEM)
    hbm = pl.BlockSpec(memory_space=pltpu.HBM)
    dma = pltpu.SemaphoreType.DMA
    grad_x, grad_h, grad_w, grad_wb = pl.pallas_call(
        lambda *refs: kernel(n_dp, *refs),
        out_shape=(
            jax.ShapeDtypeStruct((edges, width), BF16),
            jax.ShapeDtypeStruct((atoms_dev, width), BF16),
            jax.ShapeDtypeStruct((owned, width), F32),
            jax.ShapeDtypeStruct((16, 128), F32),
        ),
        in_specs=[hbm] * 11,
        out_specs=(hbm, vmem, vmem, vmem),
        scratch_shapes=[
            pltpu.VMEM((atoms_dev, width), BF16),
            pltpu.VMEM((edges, width), BF16),
            pltpu.VMEM((1, edges), jnp.int32),
            pltpu.VMEM((1, edges), jnp.int32),
            pltpu.VMEM((1, trips), jnp.int32),
            pltpu.VMEM((1, trips), jnp.int32),
            pltpu.VMEM((nb, trips), BF16),
            pltpu.SMEM((1, 1), jnp.int32),
            pltpu.VMEM((atoms_dev, width), BF16),
            pltpu.VMEM((width, width), BF16),
            pltpu.VMEM((nb, width), BF16),
            pltpu.VMEM((NX, NY, NC, 2 * atoms_dev, half), BF16),
            pltpu.VMEM((NX * NY * NC * atoms_dev, width), BF16),
            pltpu.VMEM((edges, atoms_dev * nb), BF16),
            pltpu.VMEM((atoms_dev * nb, width), BF16),
            pltpu.VMEM((edges, width), F32),
            pltpu.VMEM((edges, width), BF16),
            pltpu.VMEM((edges, width), BF16),
            pltpu.VMEM((edges, width), BF16),
            pltpu.VMEM((edges, width), BF16),
            pltpu.VMEM((NY, NX, NC, 16, 2 * width), BF16),
            pltpu.VMEM((NY, NX, NC, 16, small), BF16),
            pltpu.VMEM((NY, NX, 16, 2 * width), BF16),
            pltpu.VMEM((NY, NX, 16, small), BF16),
            pltpu.VMEM((steps, 16, 2 * width), BF16),
            pltpu.VMEM((steps, 16, small), BF16),
            pltpu.VMEM((steps, 16, 2 * width), BF16),
            pltpu.VMEM((steps, 16, small), BF16),
            pltpu.VMEM((NX, 2, 16, width), F32),
            pltpu.VMEM((NX, 16, small), F32),
            pltpu.VMEM((3, 16, width), BF16),
            pltpu.VMEM((3, 16, width), BF16),
            pltpu.VMEM((3, 16, 128), BF16),
            pltpu.VMEM((3, 16, 128), BF16),
            pltpu.VMEM((16, half), BF16),
            pltpu.VMEM((16, half), BF16),
            pltpu.VMEM((tiles + 1, 16, 128), BF16),
            pltpu.VMEM((n_dp // 2, 16, 128), BF16),
            pltpu.VMEM((2 * tiles + 1, 16, 128), BF16),
            dma((12,)),
            dma((NY,)),
            dma((NY,)),
            dma((NY,)),
            dma((NY,)),
            dma((2 * NY,)),
            dma((2 * NY,)),
            dma((2, NY)),
            dma((2, NY)),
            dma((2, steps)),
            dma((2, steps)),
            dma((2, steps)),
            dma((2, steps)),
            dma((3, 3)),
            dma((3, 3)),
            dma((tiles + 1,)),
            dma((n_dp // 2,)),
            dma((n_dp,)),
            dma((2 * tiles + 1,)),
        ],
        compiler_params=pltpu.CompilerParams(
            collective_id=0, has_side_effects=True, vmem_limit_bytes=60 * 1024 * 1024
        ),
    )(
        atom_h[0],
        edge_x[0],
        edge_source,
        edge_target,
        trip_in,
        trip_out,
        basis[0],
        block_counts,
        atom_cotangent[0],
        weight_edge,
        weight_basis,
    )
    grad_x, grad_h, grad_w, grad_wb = pl.pallas_call(
        write_out,
        out_shape=(
            jax.ShapeDtypeStruct((edges, width), BF16),
            jax.ShapeDtypeStruct((atoms_dev, width), BF16),
            jax.ShapeDtypeStruct((owned, width), F32),
            jax.ShapeDtypeStruct((owned, nb), F32),
        ),
        in_specs=[hbm] * 4,
        out_specs=(hbm, hbm, hbm, hbm),
        scratch_shapes=[
            pltpu.VMEM((edges, width), BF16),
            pltpu.VMEM((atoms_dev, width), BF16),
            pltpu.VMEM((owned, width), F32),
            pltpu.VMEM((16, 128), F32),
            pltpu.VMEM((owned, nb), F32),
            dma((7,)),
            dma((7,)),
        ],
        compiler_params=pltpu.CompilerParams(
            has_side_effects=True, vmem_limit_bytes=60 * 1024 * 1024
        ),
    )(grad_x, grad_h, grad_w, grad_wb)
    return (grad_x[None], grad_h[None], grad_w, grad_wb.T)


def solution(mesh):
    placed = (
        P("dp", "graph", None),
        P("dp", "graph", None),
        P("dp", "graph"),
        P("dp", "graph"),
        P("dp", "graph"),
        P("dp", "graph"),
        P("dp", None, "graph"),
        P("dp", "graph"),
        P("dp", "graph", None),
        P(),
        P(),
    )
    return jax.shard_map(
        shards,
        mesh=mesh,
        in_specs=placed,
        out_specs=(
            P("dp", "graph", None),
            P("dp", "graph", None),
            P("graph", None),
            P(None, "graph"),
        ),
        check_vma=False,
    )
```

```python
import jax
import jax.numpy as jnp
from jax import lax
from jax.experimental import pallas as pl
from jax.experimental.pallas import tpu as pltpu
from jax.sharding import PartitionSpec as P

BLOCK = 128
NX, NY, NC = 2, 8, 2
MESH = pl.DeviceIdType.MESH
F32 = jnp.float32
BF16 = jnp.bfloat16
TN = (((0,), (0,)), ((), ()))
NT = (((1,), (1,)), ((), ()))
DIST = (4, 3, 3, 2, 2, 1, 1)
HALF = (0, 1, 0, 1, 0, 1, 0)
PLACES = (0, -1, -2, 1, 2, -3, 3, 4)


def dot(a, b, dims=None):
    if dims is None:
        return jnp.dot(a, b, preferred_element_type=F32)
    return lax.dot_general(a, b, dims, preferred_element_type=F32)


def kernel(
    n_dp,
    h_hbm,
    x_hbm,
    src_hbm,
    tgt_hbm,
    tin_hbm,
    tout_hbm,
    basis_hbm,
    counts_hbm,
    cot_hbm,
    we_hbm,
    wb_hbm,
    gx_hbm,
    gh_ref,
    gw_ref,
    gwb_ref,
    h_ref,
    x_ref,
    src_ref,
    tgt_ref,
    tin_ref,
    tout_ref,
    basis_ref,
    counts_ref,
    cot_ref,
    we_ref,
    wb_ref,
    table,
    tab,
    mt_ref,
    g_ref,
    gm_ref,
    joined_ref,
    gp_ref,
    gx_ref,
    msg_ref,
    part_w,
    part_s,
    core_w,
    core_s,
    left_w,
    left_s,
    right_w,
    right_s,
    acc_w,
    acc_s,
    x_out_w,
    x_in_w,
    x_out_b,
    x_in_b,
    x_out_h,
    x_in_h,
    dp_out,
    dp_in,
    dp_all,
    load_sem,
    tab_send,
    tab_recv,
    tabx_send,
    tabx_recv,
    sib_send,
    sib_recv,
    core_send,
    core_recv,
    left_send,
    left_recv,
    right_send,
    right_recv,
    x_send,
    x_recv,
    dps_send,
    dps_recv,
    dpg_send,
    dpg_recv,
):
    edges, width = x_ref.shape
    nb, trips = basis_ref.shape
    atoms_dev = h_ref.shape[0]
    half = width // 2
    tiles = width // 128
    nz = n_dp // 2
    dp = lax.axis_index("dp")
    g = lax.axis_index("graph")
    chip = lax.div(g, NC)
    c = lax.rem(g, NC)
    xl = lax.div(chip, NY)
    y = lax.rem(chip, NY)
    oc = 1 - c
    xh = lax.div(dp, nz)
    z = lax.rem(dp, nz)

    def along(offset):
        return lax.rem(y + (offset + NY), NY)

    def y_peer(offset):
        return {"graph": (xl * NY + along(offset)) * NC + c}

    sibling = {"graph": chip * NC + oc}
    right, left = y_peer(1), y_peer(-1)
    other_graph = ((1 - xl) * NY + y) * NC + c
    other_dp = (1 - xh) * nz + z
    across = {"graph": other_graph}
    x_peers = (across, {"dp": other_dp}, {"dp": other_dp, "graph": other_graph})

    def signal(sem, device):
        pl.semaphore_signal(sem, inc=1, device_id=device, device_id_type=MESH)

    def remote(src, dst, send, recv, device):
        return pltpu.make_async_remote_copy(
            src_ref=src,
            dst_ref=dst,
            send_sem=send,
            recv_sem=recv,
            device_id=device,
            device_id_type=MESH,
        )

    sent = []

    def begin(copy):
        copy.start()
        sent.append(copy)

    loads = [
        pltpu.make_async_copy(src, dst, load_sem.at[i])
        for i, (src, dst) in enumerate(
            [
                (h_hbm, h_ref),
                (tout_hbm, tout_ref),
                (tgt_hbm, tgt_ref),
                (tin_hbm, tin_ref),
                (counts_hbm, counts_ref),
                (basis_hbm, basis_ref),
                (wb_hbm, wb_ref),
                (cot_hbm, cot_ref),
                (src_hbm, src_ref),
                (x_hbm, x_ref),
                (we_hbm, we_ref),
            ]
        )
    ]
    for load in loads:
        load.start()
    load_h, load_x, load_we = loads[0], loads[-2], loads[-1]

    barrier = pltpu.get_barrier_semaphore()
    greeted = [sibling, right, left, y_peer(2), y_peer(-2), across, x_peers[2]]
    for peer in greeted:
        signal(barrier, peer)

    @pl.loop(1, n_dp)
    def _(k):
        signal(barrier, {"dp": lax.rem(dp + k, n_dp)})

    load_h.wait()
    hrows = h_ref[...].astype(F32)
    own_rows = jnp.concatenate([hrows[:, :half], hrows[:, half:]], axis=0).astype(BF16)
    table[xl, y, c] = own_rows
    for load in loads[1:-2]:
        load.wait()
    edge_of_slot = lax.broadcasted_iota(jnp.int32, (edges, trips), 0)
    edge_base = g * edges
    atom_base = g * atoms_dev
    hits_out = (edge_of_slot == tout_ref[...] - edge_base).astype(F32).astype(BF16)
    target_hits = (
        (lax.broadcasted_iota(jnp.int32, (16, edges), 0) == tgt_ref[...] - atom_base)
        .astype(F32)
        .astype(BF16)
    )
    a_of = dot(target_hits, hits_out)
    slot = lax.broadcasted_iota(jnp.int32, (1, trips), 1)
    a_of = jnp.where(slot < counts_ref[0, 0] * BLOCK, a_of, 0.0)

    pl.semaphore_wait(barrier, len(greeted) + n_dp - 1)

    def block(offset, part=None):
        if part is None:
            return table.at[xl, along(offset), c]
        return table.at[xl, along(offset), c, :, part * (half // 2) : (part + 1) * (half // 2)]

    number = {-1: 0, -2: 1, 1: 2, 2: 3, -3: 4, 3: 5, -4: 6, 4: 7}
    side = {-4: 0, 4: 1}

    def table_send(offset, to):
        seen = offset - to
        i, ref = number[seen], block(offset, side.get(seen))
        begin(remote(ref, ref, tab_send.at[i], tab_recv.at[i], y_peer(to)))

    def table_wait(seen):
        i, ref = number[seen], block(seen, side.get(seen))
        remote(ref, ref, tab_send.at[i], tab_recv.at[i], sibling).wait_recv()

    def across_send(i):
        ref = block(PLACES[i])
        begin(remote(ref, ref, tabx_send.at[i], tabx_recv.at[i], across))

    def across_wait(i):
        ref = table.at[1 - xl, along(PLACES[i]), c]
        remote(ref, ref, tabx_send.at[i], tabx_recv.at[i], sibling).wait_recv()

    def sibling_send(i, other):
        ref = table.at[(1 - xl) if other else xl, along(PLACES[i]), c]
        j = other * NY + i
        begin(remote(ref, ref, sib_send.at[j], sib_recv.at[j], sibling))

    def sibling_wait(i, other):
        ref = table.at[(1 - xl) if other else xl, along(PLACES[i]), oc]
        j = other * NY + i
        remote(ref, ref, sib_send.at[j], sib_recv.at[j], sibling).wait_recv()

    for to in (2, -2, 1, -1):
        table_send(0, to)
    across_send(0)
    sibling_send(0, 0)

    for seen, to in ((-2, 1), (2, -1), (-2, 2), (2, -2)):
        if abs(to) == 1:
            table_wait(seen)
        table_send(seen, to)
    table_wait(-1)
    table_wait(1)
    for i in (2, 4, 1, 3):
        across_send(i)
    for i in (2, 4, 1, 3):
        sibling_send(i, 0)

    hits_in = (edge_of_slot == tin_ref[...] - edge_base).astype(F32).astype(BF16)
    basis = basis_ref[...].astype(F32)
    group = 256 // nb
    for q in range(atoms_dev // group):
        spreadout = jnp.concatenate(
            [basis * a_of[a : a + 1, :] for a in range(q * group, (q + 1) * group)], axis=0
        ).astype(BF16)
        mt_ref[:, q * 256 : (q + 1) * 256] = dot(hits_in, spreadout, NT).astype(BF16)

    for seen in (-3, 3, -4, 4):
        table_wait(seen)
    for i in (5, 6, 7):
        across_send(i)
    for i in (5, 6, 7):
        sibling_send(i, 0)
    for i in (0, 2, 4, 1, 3):
        across_wait(i)
        sibling_send(i, 1)

    cot = cot_ref[...].astype(F32)
    wb = wb_ref[...].astype(F32)
    for a in range(atoms_dev):
        g_ref[a * nb : (a + 1) * nb, :] = (wb * cot[a : a + 1, :]).astype(BF16)
    for j in range(width // 256):
        js = slice(j * 256, (j + 1) * 256)
        gm_ref[:, js] = dot(mt_ref[...], g_ref[:, js])

    for i in (5, 6, 7):
        across_wait(i)
        sibling_send(i, 1)
    for i in range(NY):
        sibling_wait(i, 0)
        sibling_wait(i, 1)

    all_atoms = NX * NY * NC * atoms_dev
    packed = table[...].astype(F32).reshape(NX * NY * NC, 2 * atoms_dev, half)
    tab[:, :half] = packed[:, :atoms_dev, :].reshape(all_atoms, half).astype(BF16)
    tab[:, half:] = packed[:, atoms_dev:, :].reshape(all_atoms, half).astype(BF16)

    atom_of_edge = lax.broadcasted_iota(jnp.int32, (all_atoms, edges), 0)
    hits = (
        (atom_of_edge == src_ref[...]).astype(F32) + (atom_of_edge == tgt_ref[...]).astype(F32)
    ).astype(BF16)
    load_x.wait()
    for j in range(width // 256):
        js = slice(j * 256, (j + 1) * 256)
        ends = dot(hits, tab[:, js], TN)
        joined_ref[:, js] = (x_ref[:, js].astype(F32) + ends).astype(BF16)
    load_we.wait()
    for j in range(width // 256):
        js = slice(j * 256, (j + 1) * 256)
        pre = dot(joined_ref[...], we_ref[:, js])
        logistic = 1.0 / (1.0 + jnp.exp(-pre))
        msg_ref[:, js] = (pre * logistic).astype(BF16)
        slope = logistic * (1.0 + pre * (1.0 - logistic))
        gp_ref[:, js] = (gm_ref[:, js] * slope).astype(BF16)

    def core_copy(part, landing, sem, there):
        return remote(
            part.at[there, :, oc],
            landing.at[there],
            core_send.at[sem, there],
            core_recv.at[sem, there],
            sibling,
        )

    near = lax.div(y, 4)
    for far in (1 - near, near):
        for px in range(NX):
            rows = pl.ds(pl.multiple_of((px * 2 + far) * 256, 256), 256)
            gw = dot(joined_ref[:, rows], gp_ref[...], TN).astype(BF16)
            for k in range(8):
                py = far * 4 + k // 2
                part_w[py, px, k % 2, :, :width] = gw[k * 32 : k * 32 + 16]
                part_w[py, px, k % 2, :, width:] = gw[k * 32 + 16 : k * 32 + 32]
        for m in range(4):
            begin(core_copy(part_w, core_w, 0, far * 4 + lax.rem(y + m, 4)))

    def stream(sem, part, landing, from_left, from_right):
        def add_core(offset):
            there = along(offset)
            core_copy(part, landing, sem, there).wait_recv()
            for px in range(NX):
                part[there, px, c] = (
                    part[there, px, c].astype(F32) + landing[there, px].astype(F32)
                ).astype(BF16)

        def copies(k):
            right_ref = part.at[along(DIST[k]), HALF[k], c]
            left_ref = part.at[along(-DIST[k]), 1 - HALF[k], c]
            return (
                remote(
                    right_ref, from_left.at[k], right_send.at[sem, k], right_recv.at[sem, k], right
                ),
                remote(
                    left_ref, from_right.at[k], left_send.at[sem, k], left_recv.at[sem, k], left
                ),
            )

        def step(k):
            if k == 0:
                add_core(4)
            elif k % 2:
                add_core(DIST[k])
                add_core(-DIST[k])
            to_right, to_left = copies(k)
            if k >= 2:
                before_right, before_left = copies(k - 2)
                there = along(DIST[k])
                before_right.wait_recv()
                part[there, HALF[k], c] = (
                    part[there, HALF[k], c].astype(F32) + from_left[k - 2].astype(F32)
                ).astype(BF16)
                begin(to_right)
                there = along(-DIST[k])
                before_left.wait_recv()
                part[there, 1 - HALF[k], c] = (
                    part[there, 1 - HALF[k], c].astype(F32) + from_right[k - 2].astype(F32)
                ).astype(BF16)
                begin(to_left)
            else:
                begin(to_right)
                begin(to_left)

        def finish():
            core_copy(part, landing, sem, y).wait_recv()
            for k in (5, 6):
                for copy in copies(k):
                    copy.wait_recv()
            return [
                part[y, px, c].astype(F32)
                + landing[y, px].astype(F32)
                + from_left[6 - px].astype(F32)
                + from_right[5 + px].astype(F32)
                for px in range(NX)
            ]

        return step, finish

    step_w, finish_w = stream(0, part_w, core_w, left_w, right_w)
    step_s, finish_s = stream(1, part_s, core_s, left_s, right_s)

    def owner_of(number):
        return (number // NC) % NY, number // (NC * NY), number % NC

    def basis_piece(j):
        js = slice(j * 256, (j + 1) * 256)
        spread_sum = dot(mt_ref[...], msg_ref[:, js], TN)
        gwb = jnp.zeros((nb, 256), F32)
        for a in range(atoms_dev):
            gwb = gwb + spread_sum[a * nb : (a + 1) * nb, :] * cot[a : a + 1, js]
        both = jnp.concatenate([gwb, pltpu.roll(gwb, 256 - 16, 1)], axis=0)
        turned = both.T.astype(BF16).reshape(8, 2, 16, 128)
        for k in range(8):
            py, px, pc = owner_of(j * 8 + k)
            part_s[py, px, pc, :, :128] = turned[k, 0]

    def grad_x_piece(j):
        js = slice(j * 256, (j + 1) * 256)
        gx_ref[:, js] = dot(gp_ref[...], we_ref[js, :], NT).astype(BF16)

    def atoms_piece():
        lo = dot(hits, gx_ref[:, :half])
        hi = dot(hits, gx_ref[:, half:])
        for number in range(NX * NY * NC):
            py, px, pc = owner_of(number)
            rows = slice(number * atoms_dev, (number + 1) * atoms_dev)
            part_s[py, px, pc, :, 128:] = jnp.concatenate([lo[rows], hi[rows]], axis=0).astype(
                BF16
            )

    grad_x_piece(0)
    grad_x_piece(1)
    grad_x_piece(2)
    grad_x_piece(3)
    store_gx = pltpu.make_async_copy(gx_ref, gx_hbm, load_sem.at[11])
    store_gx.start()
    atoms_piece()
    basis_piece(0)
    basis_piece(1)
    basis_piece(2)
    basis_piece(3)
    for m in (4, 3, 5, 2, 6, 1, 7, 0):
        begin(core_copy(part_s, core_s, 1, along(m - NY)))
    step_w(0)
    step_w(1)
    step_s(0)
    step_s(1)
    step_w(2)
    step_s(2)
    step_w(3)
    step_s(3)
    step_w(4)
    step_s(4)
    step_w(5)
    step_s(5)
    step_w(6)
    step_s(6)

    for px, value in enumerate(finish_w()):
        acc_w[px, 0] = value[:, :width]
        acc_w[px, 1] = value[:, width:]
    quarters = ((1 - xl, xh), (xl, 1 - xh), (1 - xl, 1 - xh))

    def x_copy(kind, p, out, landing):
        return remote(out, landing, x_send.at[kind, p], x_recv.at[kind, p], x_peers[p])

    def x_copy_w(p):
        return x_copy(0, p, x_out_w.at[p], x_in_w.at[p])

    def x_copy_b(p):
        return x_copy(1, p, x_out_b.at[p], x_in_b.at[p])

    x_copy_h = x_copy(2, 0, x_out_h, x_in_h)
    for p, (qx, qh) in enumerate(quarters):
        x_out_w[p] = acc_w[qx, qh].astype(BF16)
        begin(x_copy_w(p))
    for px, value in enumerate(finish_s()):
        acc_s[px] = value
    for p, (qx, qh) in enumerate(quarters):
        x_out_b[p] = acc_s[qx, :, :128].astype(BF16)
        begin(x_copy_b(p))
    x_out_h[...] = acc_s[1 - xl, :, 128:].astype(BF16)
    begin(x_copy_h)

    total_w = acc_w[xl, xh]
    total_b = acc_s[xl, :, :128]
    for p in range(3):
        x_copy_w(p).wait_recv()
        total_w = total_w + x_in_w[p].astype(F32)
    for p in range(3):
        x_copy_b(p).wait_recv()
        total_b = total_b + x_in_b[p].astype(F32)

    for t in range(tiles):
        dp_out[t] = total_w[:, t * 128 : (t + 1) * 128].astype(BF16)
    dp_out[tiles] = total_b.astype(BF16)
    mine = tiles + xh

    def share(t):
        return remote(
            dp_out.at[t], dp_in.at[z], dps_send.at[t], dps_recv.at[z], {"dp": xh * nz + t}
        )

    @pl.loop(0, mine)
    def _(t):
        @pl.when(t != z)
        def _():
            share(t).start()

    x_copy_h.wait_recv()
    grad_h = acc_s[xl, :, 128:] + x_in_h[...].astype(F32)
    gh_ref[...] = (
        cot + jnp.concatenate([grad_h[:atoms_dev], grad_h[atoms_dev:]], axis=1)
    ).astype(BF16)

    own_tile = xh * tiles + z

    def spread_total(k):
        return remote(
            dp_all.at[own_tile],
            dp_all.at[own_tile],
            dpg_send.at[k],
            dpg_recv.at[own_tile],
            {"dp": lax.rem(dp + k, n_dp)},
        )

    @pl.when(z < mine)
    def _():
        dp_in[z] = dp_out[z]

        @pl.loop(1, nz)
        def _(k):
            s = lax.rem(z + k, nz)
            remote(
                dp_out.at[0], dp_in.at[s], dps_send.at[0], dps_recv.at[s], sibling
            ).wait_recv()

        dp_all[own_tile] = jnp.sum(dp_in[...].astype(F32), axis=0).astype(BF16)

        @pl.loop(1, n_dp)
        def _(k):
            spread_total(k).start()

    @pl.loop(0, 2 * tiles + 1)
    def _(t):
        @pl.when(jnp.logical_or(t != own_tile, z >= mine))
        def _():
            remote(
                dp_all.at[t], dp_all.at[t], dpg_send.at[0], dpg_recv.at[t], sibling
            ).wait_recv()

    for t in range(2 * tiles):
        r, q = t // tiles, t % tiles
        gw_ref[r * 16 : (r + 1) * 16, q * 128 : (q + 1) * 128] = dp_all[t].astype(F32)
    gwb_ref[...] = dp_all[2 * tiles].astype(F32)

    @pl.when(z < mine)
    def _():
        @pl.loop(1, n_dp)
        def _(k):
            spread_total(k).wait_send()

    @pl.loop(0, mine)
    def _(t):
        @pl.when(t != z)
        def _():
            share(t).wait_send()

    for copy in sent:
        copy.wait_send()
    store_gx.wait()


def write_out(gx, gh, gw, gwb, gx_hbm, gh_hbm, gw_hbm, gwb_hbm, gx_ref, gh_ref, gw_ref, in_ref, out_ref, get, put):
    rows = gx_ref.shape[0] // 4
    nb = out_ref.shape[1]
    moves = [(gwb, in_ref, out_ref, gwb_hbm), (gh, gh_ref, gh_ref, gh_hbm), (gw, gw_ref, gw_ref, gw_hbm)]
    for i in range(4):
        part = pl.ds(i * rows, rows)
        moves.append((gx.at[part], gx_ref.at[part], gx_ref.at[part], gx_hbm.at[part]))
    gets = [pltpu.make_async_copy(a, b, get.at[i]) for i, (a, b, _, _) in enumerate(moves)]
    puts = [pltpu.make_async_copy(a, b, put.at[i]) for i, (_, _, a, b) in enumerate(moves)]
    for copy in gets:
        copy.start()
    for i, copy in enumerate(puts):
        gets[i].wait()
        if i == 0:
            out_ref[:16, :] = in_ref[:, :nb]
            out_ref[16:, :] = in_ref[:, nb:]
        copy.start()
    for copy in puts:
        copy.wait()


def shards(
    atom_h,
    edge_x,
    edge_source,
    edge_target,
    trip_in,
    trip_out,
    basis,
    block_counts,
    atom_cotangent,
    weight_edge,
    weight_basis,
):
    n_dp = lax.axis_size("dp")
    edges, width = edge_x.shape[1:]
    nb, trips = basis.shape[1:]
    atoms_dev = atom_h.shape[1]
    owned = width // (NX * NY * NC)
    half = width // 2
    small = 128 + half
    steps = len(DIST)
    tiles = width // 128
    vmem = pl.BlockSpec(memory_space=pltpu.VMEM)
    hbm = pl.BlockSpec(memory_space=pltpu.HBM)
    dma = pltpu.SemaphoreType.DMA
    grad_x, grad_h, grad_w, grad_wb = pl.pallas_call(
        lambda *refs: kernel(n_dp, *refs),
        out_shape=(
            jax.ShapeDtypeStruct((edges, width), BF16),
            jax.ShapeDtypeStruct((atoms_dev, width), BF16),
            jax.ShapeDtypeStruct((owned, width), F32),
            jax.ShapeDtypeStruct((16, 128), F32),
        ),
        in_specs=[hbm] * 11,
        out_specs=(hbm, vmem, vmem, vmem),
        scratch_shapes=[
            pltpu.VMEM((atoms_dev, width), BF16),
            pltpu.VMEM((edges, width), BF16),
            pltpu.VMEM((1, edges), jnp.int32),
            pltpu.VMEM((1, edges), jnp.int32),
            pltpu.VMEM((1, trips), jnp.int32),
            pltpu.VMEM((1, trips), jnp.int32),
            pltpu.VMEM((nb, trips), BF16),
            pltpu.SMEM((1, 1), jnp.int32),
            pltpu.VMEM((atoms_dev, width), BF16),
            pltpu.VMEM((width, width), BF16),
            pltpu.VMEM((nb, width), BF16),
            pltpu.VMEM((NX, NY, NC, 2 * atoms_dev, half), BF16),
            pltpu.VMEM((NX * NY * NC * atoms_dev, width), BF16),
            pltpu.VMEM((edges, atoms_dev * nb), BF16),
            pltpu.VMEM((atoms_dev * nb, width), BF16),
            pltpu.VMEM((edges, width), F32),
            pltpu.VMEM((edges, width), BF16),
            pltpu.VMEM((edges, width), BF16),
            pltpu.VMEM((edges, width), BF16),
            pltpu.VMEM((edges, width), BF16),
            pltpu.VMEM((NY, NX, NC, 16, 2 * width), BF16),
            pltpu.VMEM((NY, NX, NC, 16, small), BF16),
            pltpu.VMEM((NY, NX, 16, 2 * width), BF16),
            pltpu.VMEM((NY, NX, 16, small), BF16),
            pltpu.VMEM((steps, 16, 2 * width), BF16),
            pltpu.VMEM((steps, 16, small), BF16),
            pltpu.VMEM((steps, 16, 2 * width), BF16),
            pltpu.VMEM((steps, 16, small), BF16),
            pltpu.VMEM((NX, 2, 16, width), F32),
            pltpu.VMEM((NX, 16, small), F32),
            pltpu.VMEM((3, 16, width), BF16),
            pltpu.VMEM((3, 16, width), BF16),
            pltpu.VMEM((3, 16, 128), BF16),
            pltpu.VMEM((3, 16, 128), BF16),
            pltpu.VMEM((16, half), BF16),
            pltpu.VMEM((16, half), BF16),
            pltpu.VMEM((tiles + 1, 16, 128), BF16),
            pltpu.VMEM((n_dp // 2, 16, 128), BF16),
            pltpu.VMEM((2 * tiles + 1, 16, 128), BF16),
            dma((12,)),
            dma((NY,)),
            dma((NY,)),
            dma((NY,)),
            dma((NY,)),
            dma((2 * NY,)),
            dma((2 * NY,)),
            dma((2, NY)),
            dma((2, NY)),
            dma((2, steps)),
            dma((2, steps)),
            dma((2, steps)),
            dma((2, steps)),
            dma((3, 3)),
            dma((3, 3)),
            dma((tiles + 1,)),
            dma((n_dp // 2,)),
            dma((n_dp,)),
            dma((2 * tiles + 1,)),
        ],
        compiler_params=pltpu.CompilerParams(
            collective_id=0, has_side_effects=True, vmem_limit_bytes=60 * 1024 * 1024
        ),
    )(
        atom_h[0],
        edge_x[0],
        edge_source,
        edge_target,
        trip_in,
        trip_out,
        basis[0],
        block_counts,
        atom_cotangent[0],
        weight_edge,
        weight_basis,
    )
    grad_x, grad_h, grad_w, grad_wb = pl.pallas_call(
        write_out,
        out_shape=(
            jax.ShapeDtypeStruct((edges, width), BF16),
            jax.ShapeDtypeStruct((atoms_dev, width), BF16),
            jax.ShapeDtypeStruct((owned, width), F32),
            jax.ShapeDtypeStruct((owned, nb), F32),
        ),
        in_specs=[hbm] * 4,
        out_specs=(hbm, hbm, hbm, hbm),
        scratch_shapes=[
            pltpu.VMEM((edges, width), BF16),
            pltpu.VMEM((atoms_dev, width), BF16),
            pltpu.VMEM((owned, width), F32),
            pltpu.VMEM((16, 128), F32),
            pltpu.VMEM((owned, nb), F32),
            dma((7,)),
            dma((7,)),
        ],
        compiler_params=pltpu.CompilerParams(
            has_side_effects=True, vmem_limit_bytes=60 * 1024 * 1024
        ),
    )(grad_x, grad_h, grad_w, grad_wb)
    return (grad_x[None], grad_h[None], grad_w, grad_wb.T)


def solution(mesh):
    placed = (
        P("dp", "graph", None),
        P("dp", "graph", None),
        P("dp", "graph"),
        P("dp", "graph"),
        P("dp", "graph"),
        P("dp", "graph"),
        P("dp", None, "graph"),
        P("dp", "graph"),
        P("dp", "graph", None),
        P(),
        P(),
    )
    return jax.shard_map(
        shards,
        mesh=mesh,
        in_specs=placed,
        out_specs=(
            P("dp", "graph", None),
            P("dp", "graph", None),
            P("graph", None),
            P(None, "graph"),
        ),
        check_vma=False,
    )
```

```python
import jax
import jax.numpy as jnp
from jax import lax
from jax.experimental import pallas as pl
from jax.experimental.pallas import tpu as pltpu
from jax.sharding import PartitionSpec as P

BLOCK = 128
NX, NY, NC = 2, 8, 2
MESH = pl.DeviceIdType.MESH
F32 = jnp.float32
BF16 = jnp.bfloat16
TN = (((0,), (0,)), ((), ()))
NT = (((1,), (1,)), ((), ()))
DIST = (4, 3, 3, 2, 2, 1, 1)
HALF = (0, 1, 0, 1, 0, 1, 0)
PLACES = (0, -1, -2, 1, 2, -3, 3, 4)


def dot(a, b, dims=None):
    if dims is None:
        return jnp.dot(a, b, preferred_element_type=F32)
    return lax.dot_general(a, b, dims, preferred_element_type=F32)


def kernel(
    n_dp,
    h_hbm,
    x_hbm,
    src_hbm,
    tgt_hbm,
    tin_hbm,
    tout_hbm,
    basis_hbm,
    counts_hbm,
    cot_hbm,
    we_hbm,
    wb_hbm,
    gx_hbm,
    gh_ref,
    gw_ref,
    gwb_ref,
    h_ref,
    x_ref,
    src_ref,
    tgt_ref,
    tin_ref,
    tout_ref,
    basis_ref,
    counts_ref,
    cot_ref,
    we_ref,
    wb_ref,
    table,
    tab,
    mt_ref,
    g_ref,
    gm_ref,
    joined_ref,
    gp_ref,
    gx_ref,
    msg_ref,
    part_w,
    part_s,
    core_w,
    core_s,
    left_w,
    left_s,
    right_w,
    right_s,
    acc_w,
    acc_s,
    x_out_w,
    x_in_w,
    x_out_b,
    x_in_b,
    x_out_h,
    x_in_h,
    dp_out,
    dp_in,
    dp_all,
    load_sem,
    tab_send,
    tab_recv,
    tabx_send,
    tabx_recv,
    sib_send,
    sib_recv,
    core_send,
    core_recv,
    left_send,
    left_recv,
    right_send,
    right_recv,
    x_send,
    x_recv,
    dps_send,
    dps_recv,
    dpg_send,
    dpg_recv,
):
    edges, width = x_ref.shape
    nb, trips = basis_ref.shape
    atoms_dev = h_ref.shape[0]
    half = width // 2
    tiles = width // 128
    nz = n_dp // 2
    dp = lax.axis_index("dp")
    g = lax.axis_index("graph")
    chip = lax.div(g, NC)
    c = lax.rem(g, NC)
    xl = lax.div(chip, NY)
    y = lax.rem(chip, NY)
    oc = 1 - c
    xh = lax.div(dp, nz)
    z = lax.rem(dp, nz)

    def along(offset):
        return lax.rem(y + (offset + NY), NY)

    def y_peer(offset):
        return {"graph": (xl * NY + along(offset)) * NC + c}

    sibling = {"graph": chip * NC + oc}
    right, left = y_peer(1), y_peer(-1)
    other_graph = ((1 - xl) * NY + y) * NC + c
    other_dp = (1 - xh) * nz + z
    across = {"graph": other_graph}
    x_peers = (across, {"dp": other_dp}, {"dp": other_dp, "graph": other_graph})

    def signal(sem, device):
        pl.semaphore_signal(sem, inc=1, device_id=device, device_id_type=MESH)

    def remote(src, dst, send, recv, device):
        return pltpu.make_async_remote_copy(
            src_ref=src,
            dst_ref=dst,
            send_sem=send,
            recv_sem=recv,
            device_id=device,
            device_id_type=MESH,
        )

    steps_z = sorted(range(nz), key=lambda k: -min(k, nz - k))
    far_first = [(k, flip) for k in steps_z for flip in (1, 0) if k or flip]

    def z_peer(step, flip=0):
        side = (1 - xh) if flip else xh
        return {"dp": side * nz + lax.rem(z + step, nz)}

    sent = []

    def begin(copy):
        copy.start()
        sent.append(copy)

    loads = [
        pltpu.make_async_copy(src, dst, load_sem.at[i])
        for i, (src, dst) in enumerate(
            [
                (h_hbm, h_ref),
                (tout_hbm, tout_ref),
                (tgt_hbm, tgt_ref),
                (tin_hbm, tin_ref),
                (counts_hbm, counts_ref),
                (basis_hbm, basis_ref),
                (wb_hbm, wb_ref),
                (cot_hbm, cot_ref),
                (src_hbm, src_ref),
                (x_hbm, x_ref),
                (we_hbm, we_ref),
            ]
        )
    ]
    for load in loads:
        load.start()
    load_h, load_x, load_we = loads[0], loads[-2], loads[-1]

    barrier = pltpu.get_barrier_semaphore()
    greeted = [y_peer(k) for k in (4, 3, -3, 2, -2, 1, -1)] + [sibling, across, x_peers[2]]
    for peer in greeted:
        signal(barrier, peer)

    for step, flip in far_first:
        signal(barrier, z_peer(step, flip))

    load_h.wait()
    hrows = h_ref[...].astype(F32)
    own_rows = jnp.concatenate([hrows[:, :half], hrows[:, half:]], axis=0).astype(BF16)
    table[xl, y, c] = own_rows
    for load in loads[1:-2]:
        load.wait()
    edge_of_slot = lax.broadcasted_iota(jnp.int32, (edges, trips), 0)
    edge_base = g * edges
    atom_base = g * atoms_dev
    hits_out = (edge_of_slot == tout_ref[...] - edge_base).astype(F32).astype(BF16)
    target_hits = (
        (lax.broadcasted_iota(jnp.int32, (16, edges), 0) == tgt_ref[...] - atom_base)
        .astype(F32)
        .astype(BF16)
    )
    a_of = dot(target_hits, hits_out)
    slot = lax.broadcasted_iota(jnp.int32, (1, trips), 1)
    a_of = jnp.where(slot < counts_ref[0, 0] * BLOCK, a_of, 0.0)

    pl.semaphore_wait(barrier, len(greeted) + n_dp - 1)

    def block(offset):
        return table.at[xl, along(offset), c]

    def table_send(to):
        i, ref = PLACES.index(4 if to == 4 else -to), block(0)
        begin(remote(ref, ref, tab_send.at[i], tab_recv.at[i], y_peer(to)))

    def table_wait(i):
        ref = block(PLACES[i])
        remote(ref, ref, tab_send.at[i], tab_recv.at[i], sibling).wait_recv()

    def across_send(i):
        ref = block(PLACES[i])
        begin(remote(ref, ref, tabx_send.at[i], tabx_recv.at[i], across))

    def across_wait(i):
        ref = table.at[1 - xl, along(PLACES[i]), c]
        remote(ref, ref, tabx_send.at[i], tabx_recv.at[i], sibling).wait_recv()

    def sibling_send(i, other):
        ref = table.at[(1 - xl) if other else xl, along(PLACES[i]), c]
        j = other * NY + i
        begin(remote(ref, ref, sib_send.at[j], sib_recv.at[j], sibling))

    def sibling_wait(i, other):
        ref = table.at[(1 - xl) if other else xl, along(PLACES[i]), oc]
        j = other * NY + i
        remote(ref, ref, sib_send.at[j], sib_recv.at[j], sibling).wait_recv()

    for to in (4, 3, -3, 2, -2, 1, -1):
        table_send(to)
    across_send(0)
    sibling_send(0, 0)

    hits_in = (edge_of_slot == tin_ref[...] - edge_base).astype(F32).astype(BF16)
    basis = basis_ref[...].astype(F32)
    group = 256 // nb
    for q in range(atoms_dev // group):
        spreadout = jnp.concatenate(
            [basis * a_of[a : a + 1, :] for a in range(q * group, (q + 1) * group)], axis=0
        ).astype(BF16)
        mt_ref[:, q * 256 : (q + 1) * 256] = dot(hits_in, spreadout, NT).astype(BF16)

    for i in (1, 3, 2, 4, 5, 6, 7):
        table_wait(i)
        across_send(i)
        sibling_send(i, 0)

    cot = cot_ref[...].astype(F32)
    wb = wb_ref[...].astype(F32)
    for a in range(atoms_dev):
        g_ref[a * nb : (a + 1) * nb, :] = (wb * cot[a : a + 1, :]).astype(BF16)
    for j in range(width // 256):
        js = slice(j * 256, (j + 1) * 256)
        gm_ref[:, js] = dot(mt_ref[...], g_ref[:, js])

    for i in (0, 1, 3, 2, 4, 5, 6, 7):
        across_wait(i)
        sibling_send(i, 1)
    for i in range(NY):
        sibling_wait(i, 0)
        sibling_wait(i, 1)

    all_atoms = NX * NY * NC * atoms_dev
    packed = table[...].astype(F32).reshape(NX * NY * NC, 2 * atoms_dev, half)
    tab[:, :half] = packed[:, :atoms_dev, :].reshape(all_atoms, half).astype(BF16)
    tab[:, half:] = packed[:, atoms_dev:, :].reshape(all_atoms, half).astype(BF16)

    atom_of_edge = lax.broadcasted_iota(jnp.int32, (all_atoms, edges), 0)
    hits = (
        (atom_of_edge == src_ref[...]).astype(F32) + (atom_of_edge == tgt_ref[...]).astype(F32)
    ).astype(BF16)
    load_x.wait()
    for j in range(width // 256):
        js = slice(j * 256, (j + 1) * 256)
        ends = dot(hits, tab[:, js], TN)
        joined_ref[:, js] = (x_ref[:, js].astype(F32) + ends).astype(BF16)
    load_we.wait()
    for j in range(width // 256):
        js = slice(j * 256, (j + 1) * 256)
        pre = dot(joined_ref[...], we_ref[:, js])
        logistic = 1.0 / (1.0 + jnp.exp(-pre))
        msg_ref[:, js] = (pre * logistic).astype(BF16)
        slope = logistic * (1.0 + pre * (1.0 - logistic))
        gp_ref[:, js] = (gm_ref[:, js] * slope).astype(BF16)

    def core_copy(part, landing, sem, there):
        return remote(
            part.at[there, :, oc],
            landing.at[there],
            core_send.at[sem, there],
            core_recv.at[sem, there],
            sibling,
        )

    near = lax.div(y, 4)
    for far in (1 - near, near):
        for px in range(NX):
            rows = pl.ds(pl.multiple_of((px * 2 + far) * 256, 256), 256)
            gw = dot(joined_ref[:, rows], gp_ref[...], TN).astype(BF16)
            for k in range(8):
                py = far * 4 + k // 2
                part_w[py, px, k % 2, :, :width] = gw[k * 32 : k * 32 + 16]
                part_w[py, px, k % 2, :, width:] = gw[k * 32 + 16 : k * 32 + 32]
        for m in range(4):
            begin(core_copy(part_w, core_w, 0, far * 4 + lax.rem(y + m, 4)))

    def stream(sem, part, landing, from_left, from_right):
        def add_core(offset):
            there = along(offset)
            core_copy(part, landing, sem, there).wait_recv()
            for px in range(NX):
                part[there, px, c] = (
                    part[there, px, c].astype(F32) + landing[there, px].astype(F32)
                ).astype(BF16)

        def copies(k):
            right_ref = part.at[along(DIST[k]), HALF[k], c]
            left_ref = part.at[along(-DIST[k]), 1 - HALF[k], c]
            return (
                remote(
                    right_ref, from_left.at[k], right_send.at[sem, k], right_recv.at[sem, k], right
                ),
                remote(
                    left_ref, from_right.at[k], left_send.at[sem, k], left_recv.at[sem, k], left
                ),
            )

        def step(k):
            if k == 0:
                add_core(4)
            elif k % 2:
                add_core(DIST[k])
                add_core(-DIST[k])
            to_right, to_left = copies(k)
            if k >= 2:
                before_right, before_left = copies(k - 2)
                there = along(DIST[k])
                before_right.wait_recv()
                part[there, HALF[k], c] = (
                    part[there, HALF[k], c].astype(F32) + from_left[k - 2].astype(F32)
                ).astype(BF16)
                begin(to_right)
                there = along(-DIST[k])
                before_left.wait_recv()
                part[there, 1 - HALF[k], c] = (
                    part[there, 1 - HALF[k], c].astype(F32) + from_right[k - 2].astype(F32)
                ).astype(BF16)
                begin(to_left)
            else:
                begin(to_right)
                begin(to_left)

        def finish():
            core_copy(part, landing, sem, y).wait_recv()
            for k in (5, 6):
                for copy in copies(k):
                    copy.wait_recv()
            return [
                part[y, px, c].astype(F32)
                + landing[y, px].astype(F32)
                + from_left[6 - px].astype(F32)
                + from_right[5 + px].astype(F32)
                for px in range(NX)
            ]

        return step, finish

    step_w, finish_w = stream(0, part_w, core_w, left_w, right_w)
    step_s, finish_s = stream(1, part_s, core_s, left_s, right_s)

    def owner_of(number):
        return (number // NC) % NY, number // (NC * NY), number % NC

    def basis_piece(j):
        js = slice(j * 256, (j + 1) * 256)
        spread_sum = dot(mt_ref[...], msg_ref[:, js], TN)
        gwb = jnp.zeros((nb, 256), F32)
        for a in range(atoms_dev):
            gwb = gwb + spread_sum[a * nb : (a + 1) * nb, :] * cot[a : a + 1, js]
        both = jnp.concatenate([gwb, pltpu.roll(gwb, 256 - 16, 1)], axis=0)
        turned = both.T.astype(BF16).reshape(8, 2, 16, 128)
        for k in range(8):
            py, px, pc = owner_of(j * 8 + k)
            part_s[py, px, pc, :, :128] = turned[k, 0]

    def grad_x_piece(j):
        js = slice(j * 256, (j + 1) * 256)
        gx_ref[:, js] = dot(gp_ref[...], we_ref[js, :], NT).astype(BF16)

    def atoms_piece():
        lo = dot(hits, gx_ref[:, :half])
        hi = dot(hits, gx_ref[:, half:])
        for number in range(NX * NY * NC):
            py, px, pc = owner_of(number)
            rows = slice(number * atoms_dev, (number + 1) * atoms_dev)
            part_s[py, px, pc, :, 128:] = jnp.concatenate([lo[rows], hi[rows]], axis=0).astype(
                BF16
            )

    step_w(0)
    step_w(1)
    grad_x_piece(0)
    grad_x_piece(1)
    grad_x_piece(2)
    grad_x_piece(3)
    store_gx = pltpu.make_async_copy(gx_ref, gx_hbm, load_sem.at[11])
    store_gx.start()
    atoms_piece()
    basis_piece(0)
    basis_piece(1)
    basis_piece(2)
    basis_piece(3)
    for m in (4, 3, 5, 2, 6, 1, 7, 0):
        begin(core_copy(part_s, core_s, 1, along(m - NY)))
    step_s(0)
    step_s(1)
    step_w(2)
    step_s(2)
    step_w(3)
    step_s(3)
    step_s(4)
    step_w(4)
    step_s(5)
    step_w(5)
    step_s(6)
    step_w(6)

    quarters = ((1 - xl, xh), (xl, 1 - xh), (1 - xl, 1 - xh))

    def x_copy(kind, p, out, landing):
        return remote(out, landing, x_send.at[kind, p], x_recv.at[kind, p], x_peers[p])

    def x_copy_w(p):
        return x_copy(0, p, x_out_w.at[p], x_in_w.at[p])

    def x_copy_b(p):
        return x_copy(1, p, x_out_b.at[p], x_in_b.at[p])

    x_copy_h = x_copy(2, 0, x_out_h, x_in_h)
    for px, value in enumerate(finish_s()):
        acc_s[px] = value
    for p, (qx, qh) in enumerate(quarters):
        x_out_b[p] = acc_s[qx, :, :128].astype(BF16)
        begin(x_copy_b(p))
    for px, value in enumerate(finish_w()):
        acc_w[px, 0] = value[:, :width]
        acc_w[px, 1] = value[:, width:]
    for p, (qx, qh) in enumerate(quarters):
        x_out_w[p] = acc_w[qx, qh].astype(BF16)
        begin(x_copy_w(p))
    x_out_h[...] = acc_s[1 - xl, :, 128:].astype(BF16)
    begin(x_copy_h)

    total_w = acc_w[xl, xh]
    total_b = acc_s[xl, :, :128]
    for p in range(3):
        x_copy_w(p).wait_recv()
        total_w = total_w + x_in_w[p].astype(F32)
    for p in range(3):
        x_copy_b(p).wait_recv()
        total_b = total_b + x_in_b[p].astype(F32)

    for t in range(tiles):
        dp_out[t] = total_w[:, t * 128 : (t + 1) * 128].astype(BF16)
    dp_out[tiles] = total_b.astype(BF16)
    mine = tiles + xh

    def share(step):
        t = lax.rem(z + step, nz)
        return t, remote(
            dp_out.at[t], dp_in.at[z], dps_send.at[t], dps_recv.at[z], z_peer(step)
        )

    for step in steps_z[:-1]:
        tile, copy = share(step)

        @pl.when(tile < mine)
        def _(copy=copy):
            copy.start()

    x_copy_h.wait_recv()
    grad_h = acc_s[xl, :, 128:] + x_in_h[...].astype(F32)
    gh_ref[...] = (
        cot + jnp.concatenate([grad_h[:atoms_dev], grad_h[atoms_dev:]], axis=1)
    ).astype(BF16)

    own_tile = xh * tiles + z

    totals = [
        remote(
            dp_all.at[own_tile],
            dp_all.at[own_tile],
            dpg_send.at[k],
            dpg_recv.at[own_tile],
            z_peer(step, flip),
        )
        for k, (step, flip) in enumerate(far_first)
    ]

    @pl.when(z < mine)
    def _():
        dp_in[z] = dp_out[z]

        @pl.loop(1, nz)
        def _(k):
            s = lax.rem(z + k, nz)
            remote(
                dp_out.at[0], dp_in.at[s], dps_send.at[0], dps_recv.at[s], sibling
            ).wait_recv()

        dp_all[own_tile] = jnp.sum(dp_in[...].astype(F32), axis=0).astype(BF16)

        for copy in totals:
            copy.start()

    @pl.loop(0, 2 * tiles + 1)
    def _(t):
        @pl.when(jnp.logical_or(t != own_tile, z >= mine))
        def _():
            remote(
                dp_all.at[t], dp_all.at[t], dpg_send.at[0], dpg_recv.at[t], sibling
            ).wait_recv()

    for t in range(2 * tiles):
        r, q = t // tiles, t % tiles
        gw_ref[r * 16 : (r + 1) * 16, q * 128 : (q + 1) * 128] = dp_all[t].astype(F32)
    gwb_ref[...] = dp_all[2 * tiles].astype(F32)

    @pl.when(z < mine)
    def _():
        for copy in totals:
            copy.wait_send()

    for step in steps_z[:-1]:
        tile, copy = share(step)

        @pl.when(tile < mine)
        def _(copy=copy):
            copy.wait_send()

    for copy in sent:
        copy.wait_send()
    store_gx.wait()


def write_out(gx, gh, gw, gwb, gx_hbm, gh_hbm, gw_hbm, gwb_hbm, gx_ref, gh_ref, gw_ref, in_ref, out_ref, get, put):
    rows = gx_ref.shape[0] // 4
    nb = out_ref.shape[1]
    moves = [(gwb, in_ref, out_ref, gwb_hbm), (gh, gh_ref, gh_ref, gh_hbm), (gw, gw_ref, gw_ref, gw_hbm)]
    for i in range(4):
        part = pl.ds(i * rows, rows)
        moves.append((gx.at[part], gx_ref.at[part], gx_ref.at[part], gx_hbm.at[part]))
    gets = [pltpu.make_async_copy(a, b, get.at[i]) for i, (a, b, _, _) in enumerate(moves)]
    puts = [pltpu.make_async_copy(a, b, put.at[i]) for i, (_, _, a, b) in enumerate(moves)]
    for copy in gets:
        copy.start()
    for i, copy in enumerate(puts):
        gets[i].wait()
        if i == 0:
            out_ref[:16, :] = in_ref[:, :nb]
            out_ref[16:, :] = in_ref[:, nb:]
        copy.start()
    for copy in puts:
        copy.wait()


def shards(
    atom_h,
    edge_x,
    edge_source,
    edge_target,
    trip_in,
    trip_out,
    basis,
    block_counts,
    atom_cotangent,
    weight_edge,
    weight_basis,
):
    n_dp = lax.axis_size("dp")
    edges, width = edge_x.shape[1:]
    nb, trips = basis.shape[1:]
    atoms_dev = atom_h.shape[1]
    owned = width // (NX * NY * NC)
    half = width // 2
    small = 128 + half
    steps = len(DIST)
    tiles = width // 128
    vmem = pl.BlockSpec(memory_space=pltpu.VMEM)
    hbm = pl.BlockSpec(memory_space=pltpu.HBM)
    dma = pltpu.SemaphoreType.DMA
    grad_x, grad_h, grad_w, grad_wb = pl.pallas_call(
        lambda *refs: kernel(n_dp, *refs),
        out_shape=(
            jax.ShapeDtypeStruct((edges, width), BF16),
            jax.ShapeDtypeStruct((atoms_dev, width), BF16),
            jax.ShapeDtypeStruct((owned, width), F32),
            jax.ShapeDtypeStruct((16, 128), F32),
        ),
        in_specs=[hbm] * 11,
        out_specs=(hbm, vmem, vmem, vmem),
        scratch_shapes=[
            pltpu.VMEM((atoms_dev, width), BF16),
            pltpu.VMEM((edges, width), BF16),
            pltpu.VMEM((1, edges), jnp.int32),
            pltpu.VMEM((1, edges), jnp.int32),
            pltpu.VMEM((1, trips), jnp.int32),
            pltpu.VMEM((1, trips), jnp.int32),
            pltpu.VMEM((nb, trips), BF16),
            pltpu.SMEM((1, 1), jnp.int32),
            pltpu.VMEM((atoms_dev, width), BF16),
            pltpu.VMEM((width, width), BF16),
            pltpu.VMEM((nb, width), BF16),
            pltpu.VMEM((NX, NY, NC, 2 * atoms_dev, half), BF16),
            pltpu.VMEM((NX * NY * NC * atoms_dev, width), BF16),
            pltpu.VMEM((edges, atoms_dev * nb), BF16),
            pltpu.VMEM((atoms_dev * nb, width), BF16),
            pltpu.VMEM((edges, width), F32),
            pltpu.VMEM((edges, width), BF16),
            pltpu.VMEM((edges, width), BF16),
            pltpu.VMEM((edges, width), BF16),
            pltpu.VMEM((edges, width), BF16),
            pltpu.VMEM((NY, NX, NC, 16, 2 * width), BF16),
            pltpu.VMEM((NY, NX, NC, 16, small), BF16),
            pltpu.VMEM((NY, NX, 16, 2 * width), BF16),
            pltpu.VMEM((NY, NX, 16, small), BF16),
            pltpu.VMEM((steps, 16, 2 * width), BF16),
            pltpu.VMEM((steps, 16, small), BF16),
            pltpu.VMEM((steps, 16, 2 * width), BF16),
            pltpu.VMEM((steps, 16, small), BF16),
            pltpu.VMEM((NX, 2, 16, width), F32),
            pltpu.VMEM((NX, 16, small), F32),
            pltpu.VMEM((3, 16, width), BF16),
            pltpu.VMEM((3, 16, width), BF16),
            pltpu.VMEM((3, 16, 128), BF16),
            pltpu.VMEM((3, 16, 128), BF16),
            pltpu.VMEM((16, half), BF16),
            pltpu.VMEM((16, half), BF16),
            pltpu.VMEM((n_dp // 2, 16, 128), BF16),
            pltpu.VMEM((n_dp // 2, 16, 128), BF16),
            pltpu.VMEM((n_dp, 16, 128), BF16),
            dma((12,)),
            dma((NY,)),
            dma((NY,)),
            dma((NY,)),
            dma((NY,)),
            dma((2 * NY,)),
            dma((2 * NY,)),
            dma((2, NY)),
            dma((2, NY)),
            dma((2, steps)),
            dma((2, steps)),
            dma((2, steps)),
            dma((2, steps)),
            dma((3, 3)),
            dma((3, 3)),
            dma((n_dp // 2,)),
            dma((n_dp // 2,)),
            dma((n_dp,)),
            dma((n_dp,)),
        ],
        compiler_params=pltpu.CompilerParams(
            collective_id=0, has_side_effects=True, vmem_limit_bytes=60 * 1024 * 1024
        ),
    )(
        atom_h[0],
        edge_x[0],
        edge_source,
        edge_target,
        trip_in,
        trip_out,
        basis[0],
        block_counts,
        atom_cotangent[0],
        weight_edge,
        weight_basis,
    )
    grad_x, grad_h, grad_w, grad_wb = pl.pallas_call(
        write_out,
        out_shape=(
            jax.ShapeDtypeStruct((edges, width), BF16),
            jax.ShapeDtypeStruct((atoms_dev, width), BF16),
            jax.ShapeDtypeStruct((owned, width), F32),
            jax.ShapeDtypeStruct((owned, nb), F32),
        ),
        in_specs=[hbm] * 4,
        out_specs=(hbm, hbm, hbm, hbm),
        scratch_shapes=[
            pltpu.VMEM((edges, width), BF16),
            pltpu.VMEM((atoms_dev, width), BF16),
            pltpu.VMEM((owned, width), F32),
            pltpu.VMEM((16, 128), F32),
            pltpu.VMEM((owned, nb), F32),
            dma((7,)),
            dma((7,)),
        ],
        compiler_params=pltpu.CompilerParams(
            has_side_effects=True, vmem_limit_bytes=60 * 1024 * 1024
        ),
    )(grad_x, grad_h, grad_w, grad_wb)
    return (grad_x[None], grad_h[None], grad_w, grad_wb.T)


def solution(mesh):
    placed = (
        P("dp", "graph", None),
        P("dp", "graph", None),
        P("dp", "graph"),
        P("dp", "graph"),
        P("dp", "graph"),
        P("dp", "graph"),
        P("dp", None, "graph"),
        P("dp", "graph"),
        P("dp", "graph", None),
        P(),
        P(),
    )
    return jax.shard_map(
        shards,
        mesh=mesh,
        in_specs=placed,
        out_specs=(
            P("dp", "graph", None),
            P("dp", "graph", None),
            P("graph", None),
            P(None, "graph"),
        ),
        check_vma=False,
    )
```

```python
import jax
import jax.numpy as jnp
from jax import lax
from jax.experimental import pallas as pl
from jax.experimental.pallas import tpu as pltpu
from jax.sharding import PartitionSpec as P

BLOCK = 128
NX, NY, NC = 2, 8, 2
MESH = pl.DeviceIdType.MESH
F32 = jnp.float32
BF16 = jnp.bfloat16
TN = (((0,), (0,)), ((), ()))
NT = (((1,), (1,)), ((), ()))
DIST = (4, 3, 3, 2, 2, 1, 1)
HALF = (0, 1, 0, 1, 0, 1, 0)
PLACES = (0, -1, -2, 1, 2, -3, 3, 4)


def dot(a, b, dims=None):
    if dims is None:
        return jnp.dot(a, b, preferred_element_type=F32)
    return lax.dot_general(a, b, dims, preferred_element_type=F32)


def kernel(
    n_dp,
    h_hbm,
    x_hbm,
    src_hbm,
    tgt_hbm,
    tin_hbm,
    tout_hbm,
    basis_hbm,
    counts_hbm,
    cot_hbm,
    we_hbm,
    wb_hbm,
    gx_hbm,
    gh_ref,
    gw_ref,
    gwb_ref,
    h_ref,
    x_ref,
    src_ref,
    tgt_ref,
    tin_ref,
    tout_ref,
    basis_ref,
    counts_ref,
    cot_ref,
    we_ref,
    wb_ref,
    table,
    tab,
    mt_ref,
    m_ref,
    g_ref,
    gm_ref,
    joined_ref,
    gp_ref,
    gx_ref,
    msg_ref,
    part_w,
    part_b,
    part_h,
    core_w,
    core_b,
    core_h,
    left_w,
    left_b,
    left_h,
    right_w,
    right_b,
    right_h,
    acc_w,
    acc_b,
    acc_h,
    x_out_w,
    x_in_w,
    x_out_b,
    x_in_b,
    x_out_h,
    x_in_h,
    dp_out,
    dp_in,
    dp_all,
    load_sem,
    tab_send,
    tab_recv,
    tabx_send,
    tabx_recv,
    sib_send,
    sib_recv,
    core_send,
    core_recv,
    left_send,
    left_recv,
    right_send,
    right_recv,
    x_send,
    x_recv,
    dps_send,
    dps_recv,
    dpg_send,
    dpg_recv,
):
    edges, width = x_ref.shape
    nb, trips = basis_ref.shape
    atoms_dev = h_ref.shape[0]
    half = width // 2
    tiles = width // 128
    nz = n_dp // 2
    dp = lax.axis_index("dp")
    g = lax.axis_index("graph")
    chip = lax.div(g, NC)
    c = lax.rem(g, NC)
    xl = lax.div(chip, NY)
    y = lax.rem(chip, NY)
    oc = 1 - c
    xh = lax.div(dp, nz)
    z = lax.rem(dp, nz)

    def along(offset):
        return lax.rem(y + (offset + NY), NY)

    def y_peer(offset):
        return {"graph": (xl * NY + along(offset)) * NC + c}

    sibling = {"graph": chip * NC + oc}
    right, left = y_peer(1), y_peer(-1)
    other_graph = ((1 - xl) * NY + y) * NC + c
    other_dp = (1 - xh) * nz + z
    across = {"graph": other_graph}
    x_peers = (across, {"dp": other_dp}, {"dp": other_dp, "graph": other_graph})

    def signal(sem, device):
        pl.semaphore_signal(sem, inc=1, device_id=device, device_id_type=MESH)

    def remote(src, dst, send, recv, device):
        return pltpu.make_async_remote_copy(
            src_ref=src,
            dst_ref=dst,
            send_sem=send,
            recv_sem=recv,
            device_id=device,
            device_id_type=MESH,
        )

    steps_z = sorted(range(nz), key=lambda k: -min(k, nz - k))
    far_first = [(k, flip) for k in steps_z for flip in (1, 0) if k or flip]

    def z_peer(step, flip=0):
        side = (1 - xh) if flip else xh
        return {"dp": side * nz + lax.rem(z + step, nz)}

    sent = []

    def begin(copy):
        copy.start()
        sent.append(copy)

    barrier = pltpu.get_barrier_semaphore()
    greeted = [y_peer(k) for k in (4, 3, -3, 2, -2, 1, -1)] + [sibling, across, x_peers[2]]
    for peer in greeted:
        signal(barrier, peer)

    for step, flip in far_first:
        signal(barrier, z_peer(step, flip))

    loads = [
        pltpu.make_async_copy(src, dst, load_sem.at[i])
        for i, (src, dst) in enumerate(
            [
                (h_hbm, h_ref),
                (tout_hbm, tout_ref),
                (tgt_hbm, tgt_ref),
                (tin_hbm, tin_ref),
                (counts_hbm, counts_ref),
                (basis_hbm, basis_ref),
                (wb_hbm, wb_ref),
                (cot_hbm, cot_ref),
                (src_hbm, src_ref),
                (x_hbm, x_ref),
                (we_hbm, we_ref),
            ]
        )
    ]
    for load in loads:
        load.start()
    load_h, load_x, load_we = loads[0], loads[-2], loads[-1]

    load_h.wait()
    hrows = h_ref[...].astype(F32)
    own_rows = jnp.concatenate([hrows[:, :half], hrows[:, half:]], axis=0).astype(BF16)
    table[xl, y, c] = own_rows
    for load in loads[1:-2]:
        load.wait()
    edge_of_slot = lax.broadcasted_iota(jnp.int32, (edges, trips), 0)
    edge_base = g * edges
    atom_base = g * atoms_dev
    hits_out = (edge_of_slot == tout_ref[...] - edge_base).astype(F32).astype(BF16)
    target_hits = (
        (lax.broadcasted_iota(jnp.int32, (16, edges), 0) == tgt_ref[...] - atom_base)
        .astype(F32)
        .astype(BF16)
    )
    a_of = dot(target_hits, hits_out)
    slot = lax.broadcasted_iota(jnp.int32, (1, trips), 1)
    a_of = jnp.where(slot < counts_ref[0, 0] * BLOCK, a_of, 0.0)

    pl.semaphore_wait(barrier, len(greeted) + n_dp - 1)

    def block(offset):
        return table.at[xl, along(offset), c]

    def table_send(to):
        i, ref = PLACES.index(4 if to == 4 else -to), block(0)
        begin(remote(ref, ref, tab_send.at[i], tab_recv.at[i], y_peer(to)))

    def table_wait(i):
        ref = block(PLACES[i])
        remote(ref, ref, tab_send.at[i], tab_recv.at[i], sibling).wait_recv()

    def across_send(i):
        ref = block(PLACES[i])
        begin(remote(ref, ref, tabx_send.at[i], tabx_recv.at[i], across))

    def across_wait(i):
        ref = table.at[1 - xl, along(PLACES[i]), c]
        remote(ref, ref, tabx_send.at[i], tabx_recv.at[i], sibling).wait_recv()

    def sibling_send(i, other):
        ref = table.at[(1 - xl) if other else xl, along(PLACES[i]), c]
        j = other * NY + i
        begin(remote(ref, ref, sib_send.at[j], sib_recv.at[j], sibling))

    def sibling_wait(i, other):
        ref = table.at[(1 - xl) if other else xl, along(PLACES[i]), oc]
        j = other * NY + i
        remote(ref, ref, sib_send.at[j], sib_recv.at[j], sibling).wait_recv()

    for to in (4, 3, -3, 2, -2, 1, -1):
        table_send(to)
    across_send(0)
    sibling_send(0, 0)

    hits_in = (edge_of_slot == tin_ref[...] - edge_base).astype(F32).astype(BF16)
    basis = basis_ref[...].astype(F32)
    group = 256 // nb
    for q in range(atoms_dev // group):
        spreadout = jnp.concatenate(
            [basis * a_of[a : a + 1, :] for a in range(q * group, (q + 1) * group)], axis=0
        ).astype(BF16)
        mt_ref[:, q * 256 : (q + 1) * 256] = dot(hits_in, spreadout, NT).astype(BF16)
        m_ref[q * 256 : (q + 1) * 256, :] = dot(spreadout, hits_in, NT).astype(BF16)

    for i in (1, 3, 2, 4, 5, 6, 7):
        table_wait(i)
        across_send(i)
        sibling_send(i, 0)

    cot = cot_ref[...].astype(F32)
    wb = wb_ref[...].astype(F32)
    for a in range(atoms_dev):
        g_ref[a * nb : (a + 1) * nb, :] = (wb * cot[a : a + 1, :]).astype(BF16)
    for j in range(width // 256):
        js = slice(j * 256, (j + 1) * 256)
        gm_ref[:, js] = dot(mt_ref[...], g_ref[:, js])

    all_atoms = NX * NY * NC * atoms_dev
    atom_of_edge = lax.broadcasted_iota(jnp.int32, (all_atoms, edges), 0)
    ends_of = (atom_of_edge == src_ref[...]).astype(F32) + (
        atom_of_edge == tgt_ref[...]
    ).astype(F32)
    hits = ends_of.astype(BF16)
    hits_t = ends_of.T.astype(BF16)

    for i in (0, 1, 3, 2, 4, 5, 6, 7):
        across_wait(i)
        sibling_send(i, 1)
    for i in range(NY):
        sibling_wait(i, 0)
        sibling_wait(i, 1)

    packed = table[...].astype(F32).reshape(NX * NY * NC, 2 * atoms_dev, half)
    tab[:, :half] = packed[:, :atoms_dev, :].reshape(all_atoms, half).astype(BF16)
    tab[:, half:] = packed[:, atoms_dev:, :].reshape(all_atoms, half).astype(BF16)

    load_x.wait()
    for j in range(width // 256):
        js = slice(j * 256, (j + 1) * 256)
        ends = dot(hits_t, tab[:, js])
        joined_ref[:, js] = (x_ref[:, js].astype(F32) + ends).astype(BF16)
    load_we.wait()
    for j in range(width // 256):
        js = slice(j * 256, (j + 1) * 256)
        pre = dot(joined_ref[...], we_ref[:, js])
        logistic = 0.5 + 0.5 * jnp.tanh(0.5 * pre)
        msg_ref[:, js] = (pre * logistic).astype(BF16)
        slope = logistic * (1.0 + pre * (1.0 - logistic))
        gp_ref[:, js] = (gm_ref[:, js] * slope).astype(BF16)

    def core_copy(part, landing, sem, there):
        return remote(
            part.at[there, :, oc],
            landing.at[there],
            core_send.at[sem, there],
            core_recv.at[sem, there],
            sibling,
        )

    near = lax.div(y, 4)
    for far in (1 - near, near):
        for px in range(NX):
            rows = pl.ds(pl.multiple_of((px * 2 + far) * 256, 256), 256)
            gw = dot(joined_ref[:, rows], gp_ref[...], TN).astype(BF16)
            for k in range(8):
                py = far * 4 + k // 2
                part_w[py, px, k % 2, :, :width] = gw[k * 32 : k * 32 + 16]
                part_w[py, px, k % 2, :, width:] = gw[k * 32 + 16 : k * 32 + 32]
        for m in range(4):
            begin(core_copy(part_w, core_w, 0, far * 4 + lax.rem(y + m, 4)))

    def stream(sem, part, landing, from_left, from_right):
        def add_core(offset):
            there = along(offset)
            core_copy(part, landing, sem, there).wait_recv()
            for px in range(NX):
                part[there, px, c] = (
                    part[there, px, c].astype(F32) + landing[there, px].astype(F32)
                ).astype(BF16)

        def copies(k):
            right_ref = part.at[along(DIST[k]), HALF[k], c]
            left_ref = part.at[along(-DIST[k]), 1 - HALF[k], c]
            return (
                remote(
                    right_ref, from_left.at[k], right_send.at[sem, k], right_recv.at[sem, k], right
                ),
                remote(
                    left_ref, from_right.at[k], left_send.at[sem, k], left_recv.at[sem, k], left
                ),
            )

        def step(k):
            if k == 0:
                add_core(4)
            elif k % 2:
                add_core(DIST[k])
                add_core(-DIST[k])
            to_right, to_left = copies(k)
            if k >= 2:
                before_right, before_left = copies(k - 2)
                there = along(DIST[k])
                before_right.wait_recv()
                part[there, HALF[k], c] = (
                    part[there, HALF[k], c].astype(F32) + from_left[k - 2].astype(F32)
                ).astype(BF16)
                begin(to_right)
                there = along(-DIST[k])
                before_left.wait_recv()
                part[there, 1 - HALF[k], c] = (
                    part[there, 1 - HALF[k], c].astype(F32) + from_right[k - 2].astype(F32)
                ).astype(BF16)
                begin(to_left)
            else:
                begin(to_right)
                begin(to_left)

        def finish():
            core_copy(part, landing, sem, y).wait_recv()
            for k in (5, 6):
                for copy in copies(k):
                    copy.wait_recv()
            return [
                part[y, px, c].astype(F32)
                + landing[y, px].astype(F32)
                + from_left[6 - px].astype(F32)
                + from_right[5 + px].astype(F32)
                for px in range(NX)
            ]

        return step, finish

    step_w, finish_w = stream(0, part_w, core_w, left_w, right_w)
    step_b, finish_b = stream(1, part_b, core_b, left_b, right_b)
    step_h, finish_h = stream(2, part_h, core_h, left_h, right_h)

    def owner_of(number):
        return (number // NC) % NY, number // (NC * NY), number % NC

    def basis_piece(j):
        js = slice(j * 256, (j + 1) * 256)
        spread_sum = dot(m_ref[...], msg_ref[:, js])
        gwb = jnp.zeros((nb, 256), F32)
        for a in range(atoms_dev):
            gwb = gwb + spread_sum[a * nb : (a + 1) * nb, :] * cot[a : a + 1, js]
        both = jnp.concatenate([gwb, pltpu.roll(gwb, 256 - 16, 1)], axis=0)
        turned = both.T.astype(BF16).reshape(8, 2, 16, 128)
        for k in range(8):
            py, px, pc = owner_of(j * 8 + k)
            part_b[py, px, pc] = turned[k, 0]

    def grad_x_piece(j):
        js = slice(j * 256, (j + 1) * 256)
        gx_ref[:, js] = dot(gp_ref[...], we_ref[js, :], NT).astype(BF16)

    def atoms_piece():
        lo = dot(hits, gx_ref[:, :half])
        hi = dot(hits, gx_ref[:, half:])
        for number in range(NX * NY * NC):
            py, px, pc = owner_of(number)
            rows = slice(number * atoms_dev, (number + 1) * atoms_dev)
            part_h[py, px, pc] = jnp.concatenate([lo[rows], hi[rows]], axis=0).astype(BF16)

    def share_cores(sem, part, landing):
        for m in (4, 3, 5, 2, 6, 1, 7, 0):
            begin(core_copy(part, landing, sem, along(m - NY)))

    basis_piece(0)
    basis_piece(1)
    basis_piece(2)
    basis_piece(3)
    share_cores(1, part_b, core_b)
    step_w(0)
    step_w(1)
    grad_x_piece(0)
    grad_x_piece(1)
    grad_x_piece(2)
    grad_x_piece(3)
    store_gx = pltpu.make_async_copy(gx_ref, gx_hbm, load_sem.at[11])
    store_gx.start()
    atoms_piece()
    share_cores(2, part_h, core_h)
    step_b(0)
    step_b(1)
    step_w(2)
    step_b(2)
    step_h(0)
    step_w(3)
    step_b(3)
    step_h(1)
    step_b(4)
    step_w(4)
    step_b(5)
    step_h(2)
    step_w(5)
    step_b(6)
    step_h(3)
    step_w(6)

    quarters = ((1 - xl, xh), (xl, 1 - xh), (1 - xl, 1 - xh))

    def x_copy(kind, p, out, landing):
        return remote(out, landing, x_send.at[kind, p], x_recv.at[kind, p], x_peers[p])

    def x_copy_w(p):
        return x_copy(0, p, x_out_w.at[p], x_in_w.at[p])

    def x_copy_b(p):
        return x_copy(1, p, x_out_b.at[p], x_in_b.at[p])

    x_copy_h = x_copy(2, 0, x_out_h, x_in_h)
    for px, value in enumerate(finish_b()):
        acc_b[px] = value
    for p, (qx, qh) in enumerate(quarters):
        x_out_b[p] = acc_b[qx].astype(BF16)
        begin(x_copy_b(p))
    for px, value in enumerate(finish_w()):
        acc_w[px, 0] = value[:, :width]
        acc_w[px, 1] = value[:, width:]
    for p, (qx, qh) in enumerate(quarters):
        x_out_w[p] = acc_w[qx, qh].astype(BF16)
        begin(x_copy_w(p))

    total_w = acc_w[xl, xh]
    total_b = acc_b[xl]
    for p in range(3):
        x_copy_w(p).wait_recv()
        total_w = total_w + x_in_w[p].astype(F32)
    for p in range(3):
        x_copy_b(p).wait_recv()
        total_b = total_b + x_in_b[p].astype(F32)

    for t in range(tiles):
        dp_out[t] = total_w[:, t * 128 : (t + 1) * 128].astype(BF16)
    dp_out[tiles] = total_b.astype(BF16)
    mine = tiles + xh

    def share(step):
        t = lax.rem(z + step, nz)
        return t, remote(
            dp_out.at[t], dp_in.at[z], dps_send.at[t], dps_recv.at[z], z_peer(step)
        )

    for step in steps_z[:-1]:
        tile, copy = share(step)

        @pl.when(tile < mine)
        def _(copy=copy):
            copy.start()

    step_h(4)
    step_h(5)
    step_h(6)

    own_tile = xh * tiles + z

    totals = [
        remote(
            dp_all.at[own_tile],
            dp_all.at[own_tile],
            dpg_send.at[k],
            dpg_recv.at[own_tile],
            z_peer(step, flip),
        )
        for k, (step, flip) in enumerate(far_first)
    ]

    @pl.when(z < mine)
    def _():
        dp_in[z] = dp_out[z]

        @pl.loop(1, nz)
        def _(k):
            s = lax.rem(z + k, nz)
            remote(
                dp_out.at[0], dp_in.at[s], dps_send.at[0], dps_recv.at[s], sibling
            ).wait_recv()

        dp_all[own_tile] = jnp.sum(dp_in[...].astype(F32), axis=0).astype(BF16)

        for copy in totals:
            copy.start()

    for px, value in enumerate(finish_h()):
        acc_h[px] = value
    x_out_h[...] = acc_h[1 - xl].astype(BF16)
    begin(x_copy_h)

    @pl.loop(0, 2 * tiles + 1)
    def _(t):
        @pl.when(jnp.logical_or(t != own_tile, z >= mine))
        def _():
            remote(
                dp_all.at[t], dp_all.at[t], dpg_send.at[0], dpg_recv.at[t], sibling
            ).wait_recv()

    for t in range(2 * tiles):
        r, q = t // tiles, t % tiles
        gw_ref[r * 16 : (r + 1) * 16, q * 128 : (q + 1) * 128] = dp_all[t].astype(F32)
    gwb_ref[...] = dp_all[2 * tiles].astype(F32)

    x_copy_h.wait_recv()
    grad_h = acc_h[xl] + x_in_h[...].astype(F32)
    gh_ref[...] = (
        cot + jnp.concatenate([grad_h[:atoms_dev], grad_h[atoms_dev:]], axis=1)
    ).astype(BF16)

    @pl.when(z < mine)
    def _():
        for copy in totals:
            copy.wait_send()

    for step in steps_z[:-1]:
        tile, copy = share(step)

        @pl.when(tile < mine)
        def _(copy=copy):
            copy.wait_send()

    for copy in sent:
        copy.wait_send()
    store_gx.wait()


def write_out(gx, gh, gw, gwb, gx_hbm, gh_hbm, gw_hbm, gwb_hbm, gx_ref, gh_ref, gw_ref, in_ref, out_ref, get, put):
    rows = gx_ref.shape[0] // 4
    nb = out_ref.shape[1]
    moves = [(gwb, in_ref, out_ref, gwb_hbm), (gh, gh_ref, gh_ref, gh_hbm), (gw, gw_ref, gw_ref, gw_hbm)]
    for i in range(4):
        part = pl.ds(i * rows, rows)
        moves.append((gx.at[part], gx_ref.at[part], gx_ref.at[part], gx_hbm.at[part]))
    gets = [pltpu.make_async_copy(a, b, get.at[i]) for i, (a, b, _, _) in enumerate(moves)]
    puts = [pltpu.make_async_copy(a, b, put.at[i]) for i, (_, _, a, b) in enumerate(moves)]
    for copy in gets:
        copy.start()
    for i, copy in enumerate(puts):
        gets[i].wait()
        if i == 0:
            out_ref[:16, :] = in_ref[:, :nb]
            out_ref[16:, :] = in_ref[:, nb:]
        copy.start()
    for copy in puts:
        copy.wait()


def shards(
    atom_h,
    edge_x,
    edge_source,
    edge_target,
    trip_in,
    trip_out,
    basis,
    block_counts,
    atom_cotangent,
    weight_edge,
    weight_basis,
):
    n_dp = lax.axis_size("dp")
    edges, width = edge_x.shape[1:]
    nb, trips = basis.shape[1:]
    atoms_dev = atom_h.shape[1]
    owned = width // (NX * NY * NC)
    half = width // 2
    steps = len(DIST)
    tiles = width // 128
    vmem = pl.BlockSpec(memory_space=pltpu.VMEM)
    hbm = pl.BlockSpec(memory_space=pltpu.HBM)
    dma = pltpu.SemaphoreType.DMA
    grad_x, grad_h, grad_w, grad_wb = pl.pallas_call(
        lambda *refs: kernel(n_dp, *refs),
        out_shape=(
            jax.ShapeDtypeStruct((edges, width), BF16),
            jax.ShapeDtypeStruct((atoms_dev, width), BF16),
            jax.ShapeDtypeStruct((owned, width), F32),
            jax.ShapeDtypeStruct((16, 128), F32),
        ),
        in_specs=[hbm] * 11,
        out_specs=(hbm, vmem, vmem, vmem),
        scratch_shapes=[
            pltpu.VMEM((atoms_dev, width), BF16),
            pltpu.VMEM((edges, width), BF16),
            pltpu.VMEM((1, edges), jnp.int32),
            pltpu.VMEM((1, edges), jnp.int32),
            pltpu.VMEM((1, trips), jnp.int32),
            pltpu.VMEM((1, trips), jnp.int32),
            pltpu.VMEM((nb, trips), BF16),
            pltpu.SMEM((1, 1), jnp.int32),
            pltpu.VMEM((atoms_dev, width), BF16),
            pltpu.VMEM((width, width), BF16),
            pltpu.VMEM((nb, width), BF16),
            pltpu.VMEM((NX, NY, NC, 2 * atoms_dev, half), BF16),
            pltpu.VMEM((NX * NY * NC * atoms_dev, width), BF16),
            pltpu.VMEM((edges, atoms_dev * nb), BF16),
            pltpu.VMEM((atoms_dev * nb, edges), BF16),
            pltpu.VMEM((atoms_dev * nb, width), BF16),
            pltpu.VMEM((edges, width), F32),
            pltpu.VMEM((edges, width), BF16),
            pltpu.VMEM((edges, width), BF16),
            pltpu.VMEM((edges, width), BF16),
            pltpu.VMEM((edges, width), BF16),
            pltpu.VMEM((NY, NX, NC, 16, 2 * width), BF16),
            pltpu.VMEM((NY, NX, NC, 16, 128), BF16),
            pltpu.VMEM((NY, NX, NC, 16, half), BF16),
            pltpu.VMEM((NY, NX, 16, 2 * width), BF16),
            pltpu.VMEM((NY, NX, 16, 128), BF16),
            pltpu.VMEM((NY, NX, 16, half), BF16),
            pltpu.VMEM((steps, 16, 2 * width), BF16),
            pltpu.VMEM((steps, 16, 128), BF16),
            pltpu.VMEM((steps, 16, half), BF16),
            pltpu.VMEM((steps, 16, 2 * width), BF16),
            pltpu.VMEM((steps, 16, 128), BF16),
            pltpu.VMEM((steps, 16, half), BF16),
            pltpu.VMEM((NX, 2, 16, width), F32),
            pltpu.VMEM((NX, 16, 128), F32),
            pltpu.VMEM((NX, 16, half), F32),
            pltpu.VMEM((3, 16, width), BF16),
            pltpu.VMEM((3, 16, width), BF16),
            pltpu.VMEM((3, 16, 128), BF16),
            pltpu.VMEM((3, 16, 128), BF16),
            pltpu.VMEM((16, half), BF16),
            pltpu.VMEM((16, half), BF16),
            pltpu.VMEM((n_dp // 2, 16, 128), BF16),
            pltpu.VMEM((n_dp // 2, 16, 128), BF16),
            pltpu.VMEM((n_dp, 16, 128), BF16),
            dma((12,)),
            dma((NY,)),
            dma((NY,)),
            dma((NY,)),
            dma((NY,)),
            dma((2 * NY,)),
            dma((2 * NY,)),
            dma((3, NY)),
            dma((3, NY)),
            dma((3, steps)),
            dma((3, steps)),
            dma((3, steps)),
            dma((3, steps)),
            dma((3, 3)),
            dma((3, 3)),
            dma((n_dp // 2,)),
            dma((n_dp // 2,)),
            dma((n_dp,)),
            dma((n_dp,)),
        ],
        compiler_params=pltpu.CompilerParams(
            collective_id=0, has_side_effects=True, vmem_limit_bytes=60 * 1024 * 1024
        ),
    )(
        atom_h[0],
        edge_x[0],
        edge_source,
        edge_target,
        trip_in,
        trip_out,
        basis[0],
        block_counts,
        atom_cotangent[0],
        weight_edge,
        weight_basis,
    )
    grad_x, grad_h, grad_w, grad_wb = pl.pallas_call(
        write_out,
        out_shape=(
            jax.ShapeDtypeStruct((edges, width), BF16),
            jax.ShapeDtypeStruct((atoms_dev, width), BF16),
            jax.ShapeDtypeStruct((owned, width), F32),
            jax.ShapeDtypeStruct((owned, nb), F32),
        ),
        in_specs=[hbm] * 4,
        out_specs=(hbm, hbm, hbm, hbm),
        scratch_shapes=[
            pltpu.VMEM((edges, width), BF16),
            pltpu.VMEM((atoms_dev, width), BF16),
            pltpu.VMEM((owned, width), F32),
            pltpu.VMEM((16, 128), F32),
            pltpu.VMEM((owned, nb), F32),
            dma((7,)),
            dma((7,)),
        ],
        compiler_params=pltpu.CompilerParams(
            has_side_effects=True, vmem_limit_bytes=60 * 1024 * 1024
        ),
    )(grad_x, grad_h, grad_w, grad_wb)
    return (grad_x[None], grad_h[None], grad_w, grad_wb.T)


def solution(mesh):
    placed = (
        P("dp", "graph", None),
        P("dp", "graph", None),
        P("dp", "graph"),
        P("dp", "graph"),
        P("dp", "graph"),
        P("dp", "graph"),
        P("dp", None, "graph"),
        P("dp", "graph"),
        P("dp", "graph", None),
        P(),
        P(),
    )
    return jax.shard_map(
        shards,
        mesh=mesh,
        in_specs=placed,
        out_specs=(
            P("dp", "graph", None),
            P("dp", "graph", None),
            P("graph", None),
            P(None, "graph"),
        ),
        check_vma=False,
    )
```

```python
import jax
import jax.numpy as jnp
from jax import lax
from jax.experimental import pallas as pl
from jax.experimental.pallas import tpu as pltpu
from jax.sharding import PartitionSpec as P

BLOCK = 128
NX, NY, NC = 2, 8, 2
MESH = pl.DeviceIdType.MESH
F32 = jnp.float32
BF16 = jnp.bfloat16
TN = (((0,), (0,)), ((), ()))
NT = (((1,), (1,)), ((), ()))
DIST = (4, 3, 3, 2, 2, 1, 1)
HALF = (0, 1, 0, 1, 0, 1, 0)
PLACES = (0, -1, -2, 1, 2, -3, 3, 4)


def dot(a, b, dims=None):
    if dims is None:
        return jnp.dot(a, b, preferred_element_type=F32)
    return lax.dot_general(a, b, dims, preferred_element_type=F32)


def kernel(
    n_dp,
    h_hbm,
    x_hbm,
    src_hbm,
    tgt_hbm,
    tin_hbm,
    tout_hbm,
    basis_hbm,
    counts_hbm,
    cot_hbm,
    we_hbm,
    wb_hbm,
    gx_hbm,
    gh_ref,
    gw_ref,
    gwb_ref,
    h_ref,
    x_ref,
    src_ref,
    tgt_ref,
    tin_ref,
    tout_ref,
    basis_ref,
    counts_ref,
    cot_ref,
    we_ref,
    wb_ref,
    table,
    tab,
    mt_ref,
    m_ref,
    g_ref,
    gm_ref,
    joined_ref,
    gp_ref,
    gx_ref,
    msg_ref,
    part_w,
    part_b,
    part_h,
    core_w,
    core_b,
    core_h,
    left_w,
    left_b,
    left_h,
    right_w,
    right_b,
    right_h,
    acc_w,
    acc_b,
    acc_h,
    x_out_w,
    x_in_w,
    x_out_b,
    x_in_b,
    x_out_h,
    x_in_h,
    dp_out,
    dp_in,
    dp_all,
    load_sem,
    tab_send,
    tab_recv,
    tabx_send,
    tabx_recv,
    sib_send,
    sib_recv,
    core_send,
    core_recv,
    left_send,
    left_recv,
    right_send,
    right_recv,
    x_send,
    x_recv,
    dps_send,
    dps_recv,
    dpg_send,
    dpg_recv,
):
    edges, width = x_ref.shape
    nb, trips = basis_ref.shape
    atoms_dev = h_ref.shape[0]
    half = width // 2
    tiles = width // 128
    nz = n_dp // 2
    dp = lax.axis_index("dp")
    g = lax.axis_index("graph")
    chip = lax.div(g, NC)
    c = lax.rem(g, NC)
    xl = lax.div(chip, NY)
    y = lax.rem(chip, NY)
    oc = 1 - c
    xh = lax.div(dp, nz)
    z = lax.rem(dp, nz)

    def along(offset):
        return lax.rem(y + (offset + NY), NY)

    def y_peer(offset):
        return {"graph": (xl * NY + along(offset)) * NC + c}

    sibling = {"graph": chip * NC + oc}
    right, left = y_peer(1), y_peer(-1)
    other_graph = ((1 - xl) * NY + y) * NC + c
    other_dp = (1 - xh) * nz + z
    across = {"graph": other_graph}
    x_peers = (across, {"dp": other_dp}, {"dp": other_dp, "graph": other_graph})

    def signal(sem, device):
        pl.semaphore_signal(sem, inc=1, device_id=device, device_id_type=MESH)

    def remote(src, dst, send, recv, device):
        return pltpu.make_async_remote_copy(
            src_ref=src,
            dst_ref=dst,
            send_sem=send,
            recv_sem=recv,
            device_id=device,
            device_id_type=MESH,
        )

    steps_z = sorted(range(nz), key=lambda k: -min(k, nz - k))
    far_first = [(k, flip) for k in steps_z for flip in (1, 0) if k or flip]

    def z_peer(step, flip=0):
        side = (1 - xh) if flip else xh
        return {"dp": side * nz + lax.rem(z + step, nz)}

    sent = []

    def begin(copy):
        copy.start()
        sent.append(copy)

    barrier = pltpu.get_barrier_semaphore()
    greeted = [y_peer(k) for k in (4, 3, -3, 2, -2, 1, -1)] + [sibling, across, x_peers[2]]
    for peer in greeted:
        signal(barrier, peer)

    for step, flip in far_first:
        signal(barrier, z_peer(step, flip))

    loads = [
        pltpu.make_async_copy(src, dst, load_sem.at[i])
        for i, (src, dst) in enumerate(
            [
                (h_hbm, h_ref),
                (tout_hbm, tout_ref),
                (tgt_hbm, tgt_ref),
                (tin_hbm, tin_ref),
                (counts_hbm, counts_ref),
                (basis_hbm, basis_ref),
                (wb_hbm, wb_ref),
                (cot_hbm, cot_ref),
                (src_hbm, src_ref),
                (x_hbm, x_ref),
                (we_hbm, we_ref),
            ]
        )
    ]
    for load in loads:
        load.start()
    load_h, load_x, load_we = loads[0], loads[-2], loads[-1]

    load_h.wait()
    hrows = h_ref[...].astype(F32)
    own_rows = jnp.concatenate([hrows[:, :half], hrows[:, half:]], axis=0).astype(BF16)
    table[xl, y, c] = own_rows
    for load in loads[1:-2]:
        load.wait()
    edge_of_slot = lax.broadcasted_iota(jnp.int32, (edges, trips), 0)
    edge_base = g * edges
    atom_base = g * atoms_dev
    hits_out = (edge_of_slot == tout_ref[...] - edge_base).astype(F32).astype(BF16)
    target_hits = (
        (lax.broadcasted_iota(jnp.int32, (16, edges), 0) == tgt_ref[...] - atom_base)
        .astype(F32)
        .astype(BF16)
    )
    a_of = dot(target_hits, hits_out)
    slot = lax.broadcasted_iota(jnp.int32, (1, trips), 1)
    a_of = jnp.where(slot < counts_ref[0, 0] * BLOCK, a_of, 0.0)

    pl.semaphore_wait(barrier, len(greeted) + n_dp - 1)

    def block(offset):
        return table.at[xl, along(offset), c]

    def table_send(to):
        i, ref = PLACES.index(4 if to == 4 else -to), block(0)
        begin(remote(ref, ref, tab_send.at[i], tab_recv.at[i], y_peer(to)))

    def table_wait(i):
        ref = block(PLACES[i])
        remote(ref, ref, tab_send.at[i], tab_recv.at[i], sibling).wait_recv()

    def across_send(i):
        ref = block(PLACES[i])
        begin(remote(ref, ref, tabx_send.at[i], tabx_recv.at[i], across))

    def across_wait(i):
        ref = table.at[1 - xl, along(PLACES[i]), c]
        remote(ref, ref, tabx_send.at[i], tabx_recv.at[i], sibling).wait_recv()

    def sibling_send(i, other):
        ref = table.at[(1 - xl) if other else xl, along(PLACES[i]), c]
        j = other * NY + i
        begin(remote(ref, ref, sib_send.at[j], sib_recv.at[j], sibling))

    def sibling_wait(i, other):
        ref = table.at[(1 - xl) if other else xl, along(PLACES[i]), oc]
        j = other * NY + i
        remote(ref, ref, sib_send.at[j], sib_recv.at[j], sibling).wait_recv()

    for to in (4, 3, -3, 2, -2, 1, -1):
        table_send(to)
    across_send(0)
    sibling_send(0, 0)

    hits_in = (edge_of_slot == tin_ref[...] - edge_base).astype(F32).astype(BF16)
    basis = basis_ref[...].astype(F32)
    group = 256 // nb
    for q in range(atoms_dev // group):
        spreadout = jnp.concatenate(
            [basis * a_of[a : a + 1, :] for a in range(q * group, (q + 1) * group)], axis=0
        ).astype(BF16)
        mt_ref[:, q * 256 : (q + 1) * 256] = dot(hits_in, spreadout, NT).astype(BF16)
        m_ref[q * 256 : (q + 1) * 256, :] = dot(spreadout, hits_in, NT).astype(BF16)

    for i in (1, 3, 2, 4, 5, 6, 7):
        table_wait(i)
        across_send(i)
        sibling_send(i, 0)

    cot = cot_ref[...].astype(F32)
    wb = wb_ref[...].astype(F32)
    for a in range(atoms_dev):
        g_ref[a * nb : (a + 1) * nb, :] = (wb * cot[a : a + 1, :]).astype(BF16)
    for j in range(width // 256):
        js = slice(j * 256, (j + 1) * 256)
        gm_ref[:, js] = dot(mt_ref[...], g_ref[:, js])

    all_atoms = NX * NY * NC * atoms_dev
    atom_of_edge = lax.broadcasted_iota(jnp.int32, (all_atoms, edges), 0)
    ends_of = (atom_of_edge == src_ref[...]).astype(F32) + (
        atom_of_edge == tgt_ref[...]
    ).astype(F32)
    hits = ends_of.astype(BF16)
    hits_t = ends_of.T.astype(BF16)

    for i in (0, 1, 3, 2, 4, 5, 6, 7):
        across_wait(i)
        sibling_send(i, 1)
    for i in range(NY):
        sibling_wait(i, 0)
        sibling_wait(i, 1)

    packed = table[...].astype(F32).reshape(NX * NY * NC, 2 * atoms_dev, half)
    tab[:, :half] = packed[:, :atoms_dev, :].reshape(all_atoms, half).astype(BF16)
    tab[:, half:] = packed[:, atoms_dev:, :].reshape(all_atoms, half).astype(BF16)

    load_x.wait()
    for j in range(width // 256):
        js = slice(j * 256, (j + 1) * 256)
        ends = dot(hits_t, tab[:, js])
        joined_ref[:, js] = (x_ref[:, js].astype(F32) + ends).astype(BF16)
    load_we.wait()
    for j in range(width // 256):
        js = slice(j * 256, (j + 1) * 256)
        pre = dot(joined_ref[...], we_ref[:, js])
        logistic = 0.5 + 0.5 * jnp.tanh(0.5 * pre)
        msg_ref[:, js] = (pre * logistic).astype(BF16)
        slope = logistic * (1.0 + pre * (1.0 - logistic))
        gp_ref[:, js] = (gm_ref[:, js] * slope).astype(BF16)

    def core_copy(part, landing, sem, there):
        return remote(
            part.at[there, :, oc],
            landing.at[there],
            core_send.at[sem, there],
            core_recv.at[sem, there],
            sibling,
        )

    near = lax.div(y, 4)
    for far in (1 - near, near):
        for px in range(NX):
            rows = pl.ds(pl.multiple_of((px * 2 + far) * 256, 256), 256)
            gw = dot(joined_ref[:, rows], gp_ref[...], TN).astype(BF16)
            for k in range(8):
                py = far * 4 + k // 2
                part_w[py, px, k % 2, :, :width] = gw[k * 32 : k * 32 + 16]
                part_w[py, px, k % 2, :, width:] = gw[k * 32 + 16 : k * 32 + 32]
        for m in range(4):
            begin(core_copy(part_w, core_w, 0, far * 4 + lax.rem(y + m, 4)))

    def stream(sem, part, landing, from_left, from_right):
        def add_core(offset):
            there = along(offset)
            core_copy(part, landing, sem, there).wait_recv()
            for px in range(NX):
                part[there, px, c] = (
                    part[there, px, c].astype(F32) + landing[there, px].astype(F32)
                ).astype(BF16)

        def copies(k):
            right_ref = part.at[along(DIST[k]), HALF[k], c]
            left_ref = part.at[along(-DIST[k]), 1 - HALF[k], c]
            return (
                remote(
                    right_ref, from_left.at[k], right_send.at[sem, k], right_recv.at[sem, k], right
                ),
                remote(
                    left_ref, from_right.at[k], left_send.at[sem, k], left_recv.at[sem, k], left
                ),
            )

        def step(k):
            if k == 0:
                add_core(4)
            elif k % 2:
                add_core(DIST[k])
                add_core(-DIST[k])
            to_right, to_left = copies(k)
            if k >= 2:
                before_right, before_left = copies(k - 2)
                there = along(DIST[k])
                before_right.wait_recv()
                part[there, HALF[k], c] = (
                    part[there, HALF[k], c].astype(F32) + from_left[k - 2].astype(F32)
                ).astype(BF16)
                begin(to_right)
                there = along(-DIST[k])
                before_left.wait_recv()
                part[there, 1 - HALF[k], c] = (
                    part[there, 1 - HALF[k], c].astype(F32) + from_right[k - 2].astype(F32)
                ).astype(BF16)
                begin(to_left)
            else:
                begin(to_right)
                begin(to_left)

        def finish():
            core_copy(part, landing, sem, y).wait_recv()
            for k in (5, 6):
                for copy in copies(k):
                    copy.wait_recv()
            return [
                part[y, px, c].astype(F32)
                + landing[y, px].astype(F32)
                + from_left[6 - px].astype(F32)
                + from_right[5 + px].astype(F32)
                for px in range(NX)
            ]

        return step, finish

    step_w, finish_w = stream(0, part_w, core_w, left_w, right_w)
    step_b, finish_b = stream(1, part_b, core_b, left_b, right_b)
    step_h, finish_h = stream(2, part_h, core_h, left_h, right_h)

    def owner_of(number):
        return (number // NC) % NY, number // (NC * NY), number % NC

    def basis_piece(j):
        js = slice(j * 256, (j + 1) * 256)
        spread_sum = dot(m_ref[...], msg_ref[:, js])
        gwb = jnp.zeros((nb, 256), F32)
        for a in range(atoms_dev):
            gwb = gwb + spread_sum[a * nb : (a + 1) * nb, :] * cot[a : a + 1, js]
        both = jnp.concatenate([gwb, pltpu.roll(gwb, 256 - 16, 1)], axis=0)
        turned = both.T.astype(BF16).reshape(8, 2, 16, 128)
        for k in range(8):
            py, px, pc = owner_of(j * 8 + k)
            part_b[py, px, pc] = turned[k, 0]

    def grad_x_piece(j):
        js = slice(j * 256, (j + 1) * 256)
        gx_ref[:, js] = dot(gp_ref[...], we_ref[js, :], NT).astype(BF16)

    def atoms_piece():
        lo = dot(hits, gx_ref[:, :half])
        hi = dot(hits, gx_ref[:, half:])
        for number in range(NX * NY * NC):
            py, px, pc = owner_of(number)
            rows = slice(number * atoms_dev, (number + 1) * atoms_dev)
            part_h[py, px, pc] = jnp.concatenate([lo[rows], hi[rows]], axis=0).astype(BF16)

    def share_cores(sem, part, landing):
        for m in (4, 3, 5, 2, 6, 1, 7, 0):
            begin(core_copy(part, landing, sem, along(m - NY)))

    basis_piece(0)
    basis_piece(1)
    basis_piece(2)
    basis_piece(3)
    share_cores(1, part_b, core_b)
    step_w(0)
    step_w(1)
    grad_x_piece(0)
    grad_x_piece(1)
    grad_x_piece(2)
    grad_x_piece(3)
    store_gx = pltpu.make_async_copy(gx_ref, gx_hbm, load_sem.at[11])
    store_gx.start()
    atoms_piece()
    share_cores(2, part_h, core_h)
    step_b(0)
    step_b(1)
    step_w(2)
    step_b(2)
    step_h(0)
    step_w(3)
    step_b(3)
    step_h(1)
    step_b(4)
    step_w(4)
    step_b(5)
    step_h(2)
    step_w(5)
    step_b(6)
    step_h(3)
    step_w(6)

    quarters = ((1 - xl, xh), (xl, 1 - xh), (1 - xl, 1 - xh))

    def x_copy(kind, p, out, landing):
        return remote(out, landing, x_send.at[kind, p], x_recv.at[kind, p], x_peers[p])

    def x_copy_w(p):
        return x_copy(0, p, x_out_w.at[p], x_in_w.at[p])

    def x_copy_b(p):
        return x_copy(1, p, x_out_b.at[p], x_in_b.at[p])

    x_copy_h = x_copy(2, 0, x_out_h, x_in_h)
    for px, value in enumerate(finish_b()):
        acc_b[px] = value
    for p, (qx, qh) in enumerate(quarters):
        x_out_b[p] = acc_b[qx].astype(BF16)
        begin(x_copy_b(p))
    for px, value in enumerate(finish_w()):
        acc_w[px, 0] = value[:, :width]
        acc_w[px, 1] = value[:, width:]
    for p, (qx, qh) in enumerate(quarters):
        x_out_w[p] = acc_w[qx, qh].astype(BF16)
        begin(x_copy_w(p))

    total_w = acc_w[xl, xh]
    total_b = acc_b[xl]
    for p in range(3):
        x_copy_w(p).wait_recv()
        total_w = total_w + x_in_w[p].astype(F32)
    for p in range(3):
        x_copy_b(p).wait_recv()
        total_b = total_b + x_in_b[p].astype(F32)

    for t in range(tiles):
        dp_out[t] = total_w[:, t * 128 : (t + 1) * 128].astype(BF16)
    dp_out[tiles] = total_b.astype(BF16)
    mine = tiles + xh

    def share(step):
        t = lax.rem(z + step, nz)
        return t, remote(
            dp_out.at[t], dp_in.at[z], dps_send.at[t], dps_recv.at[z], z_peer(step)
        )

    for step in steps_z[:-1]:
        tile, copy = share(step)

        @pl.when(tile < mine)
        def _(copy=copy):
            copy.start()

    step_h(4)
    step_h(5)
    step_h(6)

    own_tile = xh * tiles + z

    totals = [
        remote(
            dp_all.at[own_tile],
            dp_all.at[own_tile],
            dpg_send.at[k],
            dpg_recv.at[own_tile],
            z_peer(step, flip),
        )
        for k, (step, flip) in enumerate(far_first)
    ]

    @pl.when(z < mine)
    def _():
        dp_in[z] = dp_out[z]

        @pl.loop(1, nz)
        def _(k):
            s = lax.rem(z + k, nz)
            remote(
                dp_out.at[0], dp_in.at[s], dps_send.at[0], dps_recv.at[s], sibling
            ).wait_recv()

        dp_all[own_tile] = jnp.sum(dp_in[...].astype(F32), axis=0).astype(BF16)

        for copy in totals:
            copy.start()

    for px, value in enumerate(finish_h()):
        acc_h[px] = value
    x_out_h[...] = acc_h[1 - xl].astype(BF16)
    begin(x_copy_h)

    x_copy_h.wait_recv()
    grad_h = acc_h[xl] + x_in_h[...].astype(F32)
    gh_ref[...] = (
        cot + jnp.concatenate([grad_h[:atoms_dev], grad_h[atoms_dev:]], axis=1)
    ).astype(BF16)

    for step in steps_z[:-1]:
        tile, copy = share(step)

        @pl.when(tile < mine)
        def _(copy=copy):
            copy.wait_send()

    for copy in sent:
        copy.wait_send()
    store_gx.wait()

    @pl.loop(0, 2 * tiles + 1)
    def _(t):
        @pl.when(jnp.logical_or(t != own_tile, z >= mine))
        def _():
            remote(
                dp_all.at[t], dp_all.at[t], dpg_send.at[0], dpg_recv.at[t], sibling
            ).wait_recv()

    for t in range(2 * tiles):
        r, q = t // tiles, t % tiles
        gw_ref[r * 16 : (r + 1) * 16, q * 128 : (q + 1) * 128] = dp_all[t].astype(F32)
    gwb_ref[...] = dp_all[2 * tiles].astype(F32)

    @pl.when(z < mine)
    def _():
        for copy in totals:
            copy.wait_send()


def write_out(gx, gh, gw, gwb, gx_hbm, gh_hbm, gw_hbm, gwb_hbm, gx_ref, gh_ref, gw_ref, in_ref, out_ref, get, put):
    rows = gx_ref.shape[0] // 4
    nb = out_ref.shape[1]
    moves = [(gwb, in_ref, out_ref, gwb_hbm), (gh, gh_ref, gh_ref, gh_hbm), (gw, gw_ref, gw_ref, gw_hbm)]
    for i in range(4):
        part = pl.ds(i * rows, rows)
        moves.append((gx.at[part], gx_ref.at[part], gx_ref.at[part], gx_hbm.at[part]))
    gets = [pltpu.make_async_copy(a, b, get.at[i]) for i, (a, b, _, _) in enumerate(moves)]
    puts = [pltpu.make_async_copy(a, b, put.at[i]) for i, (_, _, a, b) in enumerate(moves)]
    for copy in gets:
        copy.start()
    for i, copy in enumerate(puts):
        gets[i].wait()
        if i == 0:
            out_ref[:16, :] = in_ref[:, :nb]
            out_ref[16:, :] = in_ref[:, nb:]
        copy.start()
    for copy in puts:
        copy.wait()


def shards(
    atom_h,
    edge_x,
    edge_source,
    edge_target,
    trip_in,
    trip_out,
    basis,
    block_counts,
    atom_cotangent,
    weight_edge,
    weight_basis,
):
    n_dp = lax.axis_size("dp")
    edges, width = edge_x.shape[1:]
    nb, trips = basis.shape[1:]
    atoms_dev = atom_h.shape[1]
    owned = width // (NX * NY * NC)
    half = width // 2
    steps = len(DIST)
    tiles = width // 128
    vmem = pl.BlockSpec(memory_space=pltpu.VMEM)
    hbm = pl.BlockSpec(memory_space=pltpu.HBM)
    dma = pltpu.SemaphoreType.DMA
    grad_x, grad_h, grad_w, grad_wb = pl.pallas_call(
        lambda *refs: kernel(n_dp, *refs),
        out_shape=(
            jax.ShapeDtypeStruct((edges, width), BF16),
            jax.ShapeDtypeStruct((atoms_dev, width), BF16),
            jax.ShapeDtypeStruct((owned, width), F32),
            jax.ShapeDtypeStruct((16, 128), F32),
        ),
        in_specs=[hbm] * 11,
        out_specs=(hbm, vmem, vmem, vmem),
        scratch_shapes=[
            pltpu.VMEM((atoms_dev, width), BF16),
            pltpu.VMEM((edges, width), BF16),
            pltpu.VMEM((1, edges), jnp.int32),
            pltpu.VMEM((1, edges), jnp.int32),
            pltpu.VMEM((1, trips), jnp.int32),
            pltpu.VMEM((1, trips), jnp.int32),
            pltpu.VMEM((nb, trips), BF16),
            pltpu.SMEM((1, 1), jnp.int32),
            pltpu.VMEM((atoms_dev, width), BF16),
            pltpu.VMEM((width, width), BF16),
            pltpu.VMEM((nb, width), BF16),
            pltpu.VMEM((NX, NY, NC, 2 * atoms_dev, half), BF16),
            pltpu.VMEM((NX * NY * NC * atoms_dev, width), BF16),
            pltpu.VMEM((edges, atoms_dev * nb), BF16),
            pltpu.VMEM((atoms_dev * nb, edges), BF16),
            pltpu.VMEM((atoms_dev * nb, width), BF16),
            pltpu.VMEM((edges, width), F32),
            pltpu.VMEM((edges, width), BF16),
            pltpu.VMEM((edges, width), BF16),
            pltpu.VMEM((edges, width), BF16),
            pltpu.VMEM((edges, width), BF16),
            pltpu.VMEM((NY, NX, NC, 16, 2 * width), BF16),
            pltpu.VMEM((NY, NX, NC, 16, 128), BF16),
            pltpu.VMEM((NY, NX, NC, 16, half), BF16),
            pltpu.VMEM((NY, NX, 16, 2 * width), BF16),
            pltpu.VMEM((NY, NX, 16, 128), BF16),
            pltpu.VMEM((NY, NX, 16, half), BF16),
            pltpu.VMEM((steps, 16, 2 * width), BF16),
            pltpu.VMEM((steps, 16, 128), BF16),
            pltpu.VMEM((steps, 16, half), BF16),
            pltpu.VMEM((steps, 16, 2 * width), BF16),
            pltpu.VMEM((steps, 16, 128), BF16),
            pltpu.VMEM((steps, 16, half), BF16),
            pltpu.VMEM((NX, 2, 16, width), F32),
            pltpu.VMEM((NX, 16, 128), F32),
            pltpu.VMEM((NX, 16, half), F32),
            pltpu.VMEM((3, 16, width), BF16),
            pltpu.VMEM((3, 16, width), BF16),
            pltpu.VMEM((3, 16, 128), BF16),
            pltpu.VMEM((3, 16, 128), BF16),
            pltpu.VMEM((16, half), BF16),
            pltpu.VMEM((16, half), BF16),
            pltpu.VMEM((n_dp // 2, 16, 128), BF16),
            pltpu.VMEM((n_dp // 2, 16, 128), BF16),
            pltpu.VMEM((n_dp, 16, 128), BF16),
            dma((12,)),
            dma((NY,)),
            dma((NY,)),
            dma((NY,)),
            dma((NY,)),
            dma((2 * NY,)),
            dma((2 * NY,)),
            dma((3, NY)),
            dma((3, NY)),
            dma((3, steps)),
            dma((3, steps)),
            dma((3, steps)),
            dma((3, steps)),
            dma((3, 3)),
            dma((3, 3)),
            dma((n_dp // 2,)),
            dma((n_dp // 2,)),
            dma((n_dp,)),
            dma((n_dp,)),
        ],
        compiler_params=pltpu.CompilerParams(
            collective_id=0, has_side_effects=True, vmem_limit_bytes=60 * 1024 * 1024
        ),
    )(
        atom_h[0],
        edge_x[0],
        edge_source,
        edge_target,
        trip_in,
        trip_out,
        basis[0],
        block_counts,
        atom_cotangent[0],
        weight_edge,
        weight_basis,
    )
    grad_x, grad_h, grad_w, grad_wb = pl.pallas_call(
        write_out,
        out_shape=(
            jax.ShapeDtypeStruct((edges, width), BF16),
            jax.ShapeDtypeStruct((atoms_dev, width), BF16),
            jax.ShapeDtypeStruct((owned, width), F32),
            jax.ShapeDtypeStruct((owned, nb), F32),
        ),
        in_specs=[hbm] * 4,
        out_specs=(hbm, hbm, hbm, hbm),
        scratch_shapes=[
            pltpu.VMEM((edges, width), BF16),
            pltpu.VMEM((atoms_dev, width), BF16),
            pltpu.VMEM((owned, width), F32),
            pltpu.VMEM((16, 128), F32),
            pltpu.VMEM((owned, nb), F32),
            dma((7,)),
            dma((7,)),
        ],
        compiler_params=pltpu.CompilerParams(
            has_side_effects=True, vmem_limit_bytes=60 * 1024 * 1024
        ),
    )(grad_x, grad_h, grad_w, grad_wb)
    return (grad_x[None], grad_h[None], grad_w, grad_wb.T)


def solution(mesh):
    placed = (
        P("dp", "graph", None),
        P("dp", "graph", None),
        P("dp", "graph"),
        P("dp", "graph"),
        P("dp", "graph"),
        P("dp", "graph"),
        P("dp", None, "graph"),
        P("dp", "graph"),
        P("dp", "graph", None),
        P(),
        P(),
    )
    return jax.shard_map(
        shards,
        mesh=mesh,
        in_specs=placed,
        out_specs=(
            P("dp", "graph", None),
            P("dp", "graph", None),
            P("graph", None),
            P(None, "graph"),
        ),
        check_vma=False,
    )
```
